256 devices in a mesh: section: 4 (over x), dp: 8 (over z_hi, core), tensor: 8 (over y, z_lo).
Axes of the slice: x: 4, y: 4, z: 8 (z_hi: 4, z_lo: 2; z = z_hi * 2 + z_lo), core: 2. Of those that a mesh axis runs over, the one named last changes fastest.
Arguments:
- features: bfloat16 [6144, 8192], P(('dp', 'section'), 'tensor'), parts along dimension 0, may hold values from -6 to 6
- key_weight: bfloat16 [4, 8192, 1024], P('section', 'tensor'), may hold values from -0.0625 to 0.0625
- value_weight: bfloat16 [4, 8192, 1024], P('section', 'tensor'), may hold values from -0.0625 to 0.0625
- queries: bfloat16 [4, 2048, 8192], P('section', 'dp', 'tensor'), parts along dimension 1, may hold values from -60 to 60
- out_grad: bfloat16 [4, 2048, 8192], P('section', 'dp', 'tensor'), parts along dimension 1, may hold values from -6 to 6
- tile_count: int32 [32], P('dp'), parts along dimension 0, may hold values from 96 to 192, as said below
- tile_last: int32 [2048], P('dp'), parts along dimension 0, may hold values from 0 to 3, as said below
Outputs:
- attended: bfloat16 [4, 2048, 8192], P('section', 'dp', 'tensor'), parts along dimension 1
- feature_grad: bfloat16 [6144, 8192], P(('dp', 'section'), 'tensor'), parts along dimension 0
- key_weight_grad: bfloat16 [4, 8192, 8192], P('section', 'tensor', 'dp'), parts along dimension 2
- value_weight_grad: bfloat16 [4, 8192, 8192], P('section', 'tensor', 'dp'), parts along dimension 2
The draws below stay inside these ranges and needn't reach their ends.
There are 8 independent parts, one for each index of `dp`. The reference program is written for one: setup_inputs(seed, part) draws one part's arguments, and reference() takes and returns one part's arrays. A program takes and returns all parts, laid end to end along the dimension named above; an argument that names none is the same for every part. Nothing has to cross between parts.
Inputs may be any that keep to these rules, and one draw needn't show every extreme that they name: `tile_count`: each tile has between 96 and 192 image tokens; some tile is full. `tile_last`: every text token sees tile 0; some token sees every tile.
All inputs are finite; a program needn't handle non-finite values.
Results may differ from the reference program's by a relative error of at most 0.015.
The reference program's roundings to bfloat16 on the way count: a program that leaves them out, or rounds other values in their place, can miss the bound.
Values may be sent and summed in bfloat16 or wider, within the bound.
A program may use at most 128 MiB of HBM per device.

```python
import jax
import jax.numpy as jnp
from jax import lax

D = 8192
HQ = 64
KVH = 8
HD = 128
TILE = 192
S = 256
IMG = 768
N_SECTION = 4


def draw_queries(key, part):
    key = jax.random.fold_in(key, 11)
    first = jax.random.fold_in(key, 0)
    shape = (N_SECTION, S, HQ * HD)
    base = jnp.clip(jax.random.normal(first, shape, jnp.float32), -6.0, 6.0)
    return base.astype(jnp.bfloat16)


def draw_tile_count(key, part):
    key = jax.random.fold_in(key, 21)
    first, second = jax.random.split(key, 2)
    counts = jax.random.randint(first, (N_SECTION,), TILE // 2, TILE + 1)
    full = (part + jax.random.randint(second, (), 0, N_SECTION)) % N_SECTION
    return jnp.where(jnp.arange(N_SECTION) == full, TILE, counts).astype(jnp.int32)


def draw_tile_last(key, part):
    key = jax.random.fold_in(key, 31)
    first, second, third = jax.random.split(key, 3)
    lasts = jax.random.randint(first, (S,), 0, N_SECTION)
    high = jax.random.randint(second, (), 0, S)
    low = (high + 1 + jax.random.randint(third, (), 0, S - 1)) % S
    lasts = lasts.at[high].set(N_SECTION - 1)
    lasts = lasts.at[low].set(0)
    return lasts.astype(jnp.int32)


def level_of(rng, extent, pieces, least, top_value):
    gain = 1.0
    for axis_at, shards_of in pieces:
        heights = jax.random.uniform(jax.random.fold_in(jax.random.fold_in(rng, 6), axis_at), (shards_of,), jnp.float32, least / len(pieces), top_value / len(pieces))
        gain = gain * jnp.repeat(jnp.exp(heights), extent[axis_at] // shards_of).reshape((-1,) + (1,) * (len(extent) - 1 - axis_at))
    return gain


def noise(key, extent, spread, most, pieces=(), kind=jnp.bfloat16):
    values = spread * jax.random.normal(key, extent, jnp.float32)
    if pieces:
        values = values * level_of(key, extent, pieces, -0.22, 0.18)
    return jnp.clip(values, -most, most).astype(kind)


def setup_inputs(seed: int = 0, part: int = 0) -> dict:
    key_of = jax.random.split(jax.random.key(seed), 8)
    part_splits = jax.random.split(jax.random.fold_in(key_of[7], part), 8)
    return {
        "features": noise(part_splits[0], (IMG, D), 1.0, 6.0, ((0, 4), (1, 8))),
        "key_weight": noise(key_of[1], (N_SECTION, D, KVH * HD), D ** -0.5, 0.0625, ((0, 4), (1, 8))),
        "value_weight": noise(key_of[2], (N_SECTION, D, KVH * HD), D ** -0.5, 0.0625, ((0, 4), (1, 8))),
        "queries": draw_queries(jax.random.fold_in(jax.random.fold_in(key_of[7], part), 71), part),
        "out_grad": noise(part_splits[4], (N_SECTION, S, HQ * HD), 1.0, 6.0, ((0, 4), (2, 8))),
        "tile_count": draw_tile_count(jax.random.fold_in(jax.random.fold_in(key_of[7], part), 71), part),
        "tile_last": draw_tile_last(jax.random.fold_in(jax.random.fold_in(key_of[7], part), 71), part),
    }


def visibility(tile_count, tile_last, tile, sections):
    slots = jnp.arange(tile * sections, dtype=jnp.int32)
    tile_of = slots // tile
    slot_in = slots % tile
    present = slot_in < tile_count[tile_of]
    return (present[None, :] & (tile_of[None, :] <= tile_last[:, None])).astype(jnp.int32)


def one_layer(features, visible, key_w, value_w, query, dout):
    img = features.shape[0]
    seq = query.shape[0]
    group = HQ // KVH
    scale = HD ** -0.5
    keys = jnp.dot(features, key_w, preferred_element_type=jnp.float32).astype(jnp.bfloat16)
    values = jnp.dot(features, value_w, preferred_element_type=jnp.float32).astype(jnp.bfloat16)
    qf = query.astype(jnp.float32).reshape(seq, KVH, group, HD)
    kf = keys.astype(jnp.float32).reshape(img, KVH, HD)
    vf = values.astype(jnp.float32).reshape(img, KVH, HD)
    scores = jnp.einsum('skgd,jkd->kgsj', qf, kf) * scale
    masked = jnp.where(visible[None, None] > 0, scores, -jnp.inf)
    top = jnp.max(masked, axis=-1, keepdims=True)
    expo = jnp.exp(masked - top)
    probs = expo / jnp.sum(expo, axis=-1, keepdims=True)
    probs16 = probs.astype(jnp.bfloat16)
    pf = probs16.astype(jnp.float32)
    out = jnp.einsum('kgsj,jkd->skgd', pf, vf).reshape(seq, HQ * HD).astype(jnp.bfloat16)
    gf = dout.astype(jnp.float32).reshape(seq, KVH, group, HD)
    dprobs = jnp.einsum('skgd,jkd->kgsj', gf, vf)
    delta = jnp.sum(probs * dprobs, axis=-1, keepdims=True)
    dscores = (probs * (dprobs - delta) * scale).astype(jnp.bfloat16)
    dkeys = jnp.einsum('kgsj,skgd->jkd', dscores.astype(jnp.float32), qf).reshape(img, KVH * HD).astype(jnp.bfloat16)
    dvalues = jnp.einsum('kgsj,skgd->jkd', pf, gf).reshape(img, KVH * HD).astype(jnp.bfloat16)
    key_grad = jnp.dot(features.T, dkeys, preferred_element_type=jnp.float32).astype(jnp.bfloat16)
    value_grad = jnp.dot(features.T, dvalues, preferred_element_type=jnp.float32).astype(jnp.bfloat16)
    fgrad = jnp.dot(dkeys, key_w.T, preferred_element_type=jnp.float32) + jnp.dot(dvalues, value_w.T, preferred_element_type=jnp.float32)
    return out, key_grad, value_grad, fgrad


def reference(features, key_weight, value_weight, queries, out_grad, tile_count, tile_last):
    sections = key_weight.shape[0]
    tile = features.shape[0] // sections
    visible = visibility(tile_count, tile_last, tile, sections)

    def layer(operands):
        return one_layer(features, visible, operands[0], operands[1], operands[2], operands[3])

    out, key_grad, value_grad, fgrad = lax.map(layer, (key_weight, value_weight, queries, out_grad))
    feature_grad = jnp.sum(fgrad, axis=0).astype(jnp.bfloat16)
    return out, feature_grad, key_grad, value_grad
```

```python
import functools

import jax
import jax.numpy as jnp
from jax import lax
from jax.experimental import pallas as pl
from jax.experimental.pallas import tpu as pltpu
from jax.sharding import PartitionSpec as P

MESH = pl.DeviceIdType.MESH
F32 = jnp.float32
BF16 = jnp.bfloat16
I16 = jnp.int16
HD = 128
GROUP = 8
SECTIONS = 4
RING = 4
TILE = 192
CODED = TILE + 16
DEPTH = 1024
SEQ = 256
LEVELS = 32700.0
VMEM_LIMIT = 56 * 2**20


def place():
    t = lax.axis_index("tensor")
    return lax.axis_index("section"), lax.axis_index("dp"), t // 2, lax.rem(t, 2)


def along_x(d):
    s, dp, y, z = place()
    return (lax.rem(s + d, SECTIONS), dp, y * 2 + z)


def along_y(d):
    s, dp, y, z = place()
    return (s, dp, lax.rem(y + d, RING) * 2 + z)


def along_z():
    s, dp, y, z = place()
    return (s, dp, y * 2 + (1 - z))


def meet():
    barrier = pltpu.get_barrier_semaphore()
    peers = [along_x(d) for d in (1, 2, 3)] + [along_y(d) for d in (1, 2, 3)] + [along_z()]
    for peer in peers:
        pl.semaphore_signal(barrier, inc=1, device_id=peer, device_id_type=MESH)
    pl.semaphore_wait(barrier, len(peers))


def remote(src, dst, send_sem, recv_sem, device):
    return pltpu.make_async_remote_copy(
        src_ref=src, dst_ref=dst, send_sem=send_sem, recv_sem=recv_sem,
        device_id=device, device_id_type=MESH,
    )


def encode(x):
    top = jnp.maximum(jnp.max(jnp.abs(x), axis=0, keepdims=True), 1e-30)
    power = jnp.ceil(jnp.log(top) * 1.4426950408889634 + 0.0005)
    code = jnp.round(x * (jnp.exp2(-power) * LEVELS)).astype(jnp.int32).astype(I16)
    mark = jnp.broadcast_to(power, (16, x.shape[1])).astype(jnp.int32).astype(I16)
    return code, mark


def put(ref, at, x):
    code, mark = encode(x)
    ref[at + (slice(0, TILE), slice(None))] = code
    ref[at + (slice(TILE, CODED), slice(None))] = mark


def get(ref, at):
    code = ref[at + (slice(0, TILE), slice(None))].astype(jnp.int32).astype(F32)
    mark = ref[at + (slice(TILE, CODED), slice(None))].astype(jnp.int32).astype(F32)
    return code * (jnp.exp2(mark[:1]) * (1.0 / LEVELS))


def project_kernel(
    f_ref, wk_ref, wv_ref, keys_ref, values_ref, ft_ref,
    fg, pk, pv, kz_out, kz_in, ky_out, ky_in, vy_out, vy_in, vz_out, vz_in, sv,
    x_send, x_recv, kz_send, kz_recv, ky_send, ky_recv, vy_send, vy_recv, vz_send, vz_recv,
):
    s, dp, y, z = place()
    meet()
    sends = []
    gathers = {}
    for d in (1, 3, 2):
        k = SECTIONS - d
        gathers[k] = remote(f_ref, fg.at[k], x_send.at[k], x_recv.at[k], along_x(d))
        gathers[k].start()
        sends.append(gathers[k])

    first_k, first_v, second_k, second_v = {}, {}, {}, {}

    def start(k):
        if k:
            gathers[k].wait_recv()
            tile = fg[k]
        else:
            tile = f_ref[...]
        v = jnp.dot(tile, wv_ref[...], preferred_element_type=F32)
        for h in range(8):
            pv[k, h] = v[:, h * HD:(h + 1) * HD]
        for d in (2, 1, 3):
            for r in range(2):
                head = lax.rem(y + d, RING) * 2 + lax.rem(z + r, 2)
                put(vy_out, (k, d, r), pv[k, head])
            copy = remote(
                vy_out.at[k, d], vy_in.at[k, RING - d],
                vy_send.at[k, d], vy_recv.at[k, RING - d], along_y(d),
            )
            copy.start()
            first_v[k, d] = copy
            sends.append(copy)
        q = jnp.dot(tile, wk_ref[...], preferred_element_type=F32)
        for h in range(8):
            pk[k, h] = q[:, h * HD:(h + 1) * HD]
        for d in range(RING):
            head = lax.rem(y + d, RING) * 2 + (1 - z)
            put(kz_out, (k, d), pk[k, head])
        copy = remote(kz_out.at[k], kz_in.at[k], kz_send.at[k], kz_recv.at[k], along_z())
        copy.start()
        first_k[k] = copy
        sends.append(copy)
        ft_ref[k] = tile.T

    def middle(k):
        first_k[k].wait_recv()
        for d in (2, 1, 3, 0):
            head = lax.rem(y + d, RING) * 2 + z
            total = pk[k, head] + get(kz_in, (k, d))
            if d:
                put(ky_out, (k, d), total)
                copy = remote(
                    ky_out.at[k, d], ky_in.at[k, RING - d],
                    ky_send.at[k, d], ky_recv.at[k, RING - d], along_y(d),
                )
                copy.start()
                second_k[k, d] = copy
                sends.append(copy)
            else:
                pk[k, head] = total
        for d in (1, 3, 2):
            first_v[k, RING - d].wait_recv()
        for r in (1, 0):
            head = y * 2 + lax.rem(z + r, 2)
            total = pv[k, head]
            for d in (1, 2, 3):
                total = total + get(vy_in, (k, d, r))
            if r:
                put(vz_out, (k,), total)
                copy = remote(vz_out.at[k], vz_in.at[k], vz_send.at[k], vz_recv.at[k], along_z())
                copy.start()
                second_v[k] = copy
                sends.append(copy)
            else:
                sv[k] = total

    def finish(k):
        for d in (1, 3, 2):
            second_k[k, RING - d].wait_recv()
        total = pk[k, y * 2 + z]
        for d in (1, 2, 3):
            total = total + get(ky_in, (k, d))
        keys_ref[k] = total.astype(BF16)
        second_v[k].wait_recv()
        values_ref[k] = (sv[k] + get(vz_in, (k,))).astype(BF16)

    order = (0, 1, 3, 2)
    for i in range(len(order) + 2):
        if i < len(order):
            start(order[i])
        if 0 <= i - 1 < len(order):
            middle(order[i - 1])
        if 0 <= i - 2:
            finish(order[i - 2])
    for copy in sends:
        copy.wait_send()


def project(f, wk, wv):
    dma = pltpu.SemaphoreType.DMA
    return pl.pallas_call(
        project_kernel,
        out_shape=(
            jax.ShapeDtypeStruct((4, TILE, HD), BF16),
            jax.ShapeDtypeStruct((4, TILE, HD), BF16),
            jax.ShapeDtypeStruct((4, DEPTH, TILE), BF16),
        ),
        in_specs=[pl.BlockSpec(memory_space=pltpu.VMEM)] * 3,
        out_specs=(pl.BlockSpec(memory_space=pltpu.VMEM),) * 3,
        scratch_shapes=[
            pltpu.VMEM((4, TILE, DEPTH), BF16),
            pltpu.VMEM((4, 8, TILE, HD), F32),
            pltpu.VMEM((4, 8, TILE, HD), F32),
            pltpu.VMEM((4, 4, CODED, HD), I16),
            pltpu.VMEM((4, 4, CODED, HD), I16),
            pltpu.VMEM((4, 4, CODED, HD), I16),
            pltpu.VMEM((4, 4, CODED, HD), I16),
            pltpu.VMEM((4, 4, 2, CODED, HD), I16),
            pltpu.VMEM((4, 4, 2, CODED, HD), I16),
            pltpu.VMEM((4, CODED, HD), I16),
            pltpu.VMEM((4, CODED, HD), I16),
            pltpu.VMEM((4, TILE, HD), F32),
            dma((4,)), dma((4,)),
            dma((4,)), dma((4,)),
            dma((4, 4)), dma((4, 4)),
            dma((4, 4)), dma((4, 4)),
            dma((4,)), dma((4,)),
        ],
        compiler_params=pltpu.CompilerParams(
            collective_id=1, has_side_effects=True, vmem_limit_bytes=VMEM_LIMIT
        ),
        name="project",
    )(f, wk, wv)


def attend_kernel(q_ref, g_ref, k_ref, v_ref, lim_ref, last_ref, out_ref, dk_ref, dv_ref, acc_k, acc_v):
    scale = HD ** -0.5
    rows = 4 * TILE
    keys = k_ref[...]
    values = v_ref[...]
    values_t = values.T
    visible = lim_ref[...] <= last_ref[...]
    across = (((1,), (1,)), ((), ()))
    for h in range(GROUP):
        cols = slice(h * HD, (h + 1) * HD)
        q = q_ref[:, cols]
        g = g_ref[:, cols]
        scores = lax.dot_general(keys, q, across, preferred_element_type=F32) * scale
        masked = jnp.where(visible, scores, -jnp.inf)
        top = jnp.max(masked, axis=0, keepdims=True)
        expo = jnp.exp(masked - top)
        probs = expo * (1.0 / jnp.sum(expo, axis=0, keepdims=True))
        probs16 = probs.astype(BF16)
        out_t = jnp.dot(values_t, probs16, preferred_element_type=F32)
        out_ref[:, cols] = out_t.T.astype(BF16)
        dprobs = lax.dot_general(values, g, across, preferred_element_type=F32)
        delta = jnp.sum(probs * dprobs, axis=0, keepdims=True)
        dscores = (probs * (dprobs - delta) * scale).astype(BF16)
        dv = jnp.dot(probs16, g, preferred_element_type=F32)
        dk = jnp.dot(dscores, q, preferred_element_type=F32)
        if h == 0:
            acc_k[...] = dk
            acc_v[...] = dv
        else:
            acc_k[...] += dk
            acc_v[...] += dv
    dk_ref[...] = acc_k[...].astype(BF16)
    dv_ref[...] = acc_v[...].astype(BF16)


def attend(q, g, keys, values, lim, last):
    rows = 4 * TILE
    return pl.pallas_call(
        attend_kernel,
        out_shape=(
            jax.ShapeDtypeStruct((SEQ, GROUP * HD), BF16),
            jax.ShapeDtypeStruct((rows, HD), BF16),
            jax.ShapeDtypeStruct((rows, HD), BF16),
        ),
        in_specs=[pl.BlockSpec(memory_space=pltpu.VMEM)] * 6,
        out_specs=(pl.BlockSpec(memory_space=pltpu.VMEM),) * 3,
        scratch_shapes=[pltpu.VMEM((rows, HD), F32), pltpu.VMEM((rows, HD), F32)],
        compiler_params=pltpu.CompilerParams(vmem_limit_bytes=VMEM_LIMIT),
        name="attend",
    )(q, g, keys, values, lim, last)


def spread_kernel(
    dk_ref, dv_ref, ft_ref, wk_ref, wv_ref, fgrad_ref, kgrad_ref, vgrad_ref,
    gk, gv, fs, fr, acc_f, acc_k, acc_v,
    own, k1s, k1r, k2s, k2r, v1s, v1r, v2s, v2r, zs, zr, xs, xr,
):
    s, dp, y, z = place()
    me = y * 2 + z

    def cols(head):
        return pl.ds(pl.multiple_of(head * HD, HD), HD)

    mine = cols(me)
    mate = cols(y * 2 + (1 - z))
    meet()
    sends = []
    owned, near, seen = {}, {}, {}

    def first(k):
        for j, (src, dst) in enumerate(((dk_ref, gk), (dv_ref, gv))):
            copy = pltpu.make_async_copy(src.at[k], dst.at[k, :, mine], own.at[k, j])
            copy.start()
            owned[k, j] = copy
        copy = remote(dk_ref.at[k], gk.at[k, :, mine], zs.at[k, 0], zr.at[k, 0], along_z())
        copy.start()
        near[k, "z"] = copy
        for d in (2, 1, 3):
            copy = remote(dv_ref.at[k], gv.at[k, :, mine], v1s.at[k, d], v1r.at[k, RING - d], along_y(d))
            copy.start()
            near[k, RING - d] = copy
        for d in (2, 1, 3):
            copy = remote(dk_ref.at[k], gk.at[k, :, mine], k1s.at[k, d], k1r.at[k, RING - d], along_y(d))
            copy.start()
            seen[k, "k1", RING - d] = copy
        copy = remote(dv_ref.at[k], gv.at[k, :, mine], zs.at[k, 1], zr.at[k, 1], along_z())
        copy.start()
        seen[k, "z1"] = copy

    def second(k):
        near[k, "z"].wait_recv()
        for d in (2, 1, 3):
            copy = remote(gk.at[k, :, mate], gk.at[k, :, mate], k2s.at[k, d], k2r.at[k, RING - d], along_y(d))
            copy.start()
            seen[k, "k2", RING - d] = copy
        for d in (1, 3, 2):
            near[k, d].wait_recv()
            head = cols(lax.rem(y + d, RING) * 2 + z)
            copy = remote(gv.at[k, :, head], gv.at[k, :, head], v2s.at[k, d], v2r.at[k, d], along_z())
            copy.start()
            seen[k, "v2", d] = copy

    across = (((1,), (1,)), ((), ()))
    parts = []

    def third(k, begin):
        owned[k, 0].wait()
        owned[k, 1].wait()
        for name, copy in seen.items():
            if name[0] == k:
                copy.wait_recv()
        total = lax.dot_general(gk[k], wk_ref[...], across, preferred_element_type=F32)
        total += lax.dot_general(gv[k], wv_ref[...], across, preferred_element_type=F32)
        if k:
            fs[k] = total.astype(BF16)
            copy = remote(fs.at[k], fr.at[SECTIONS - k], xs.at[k], xr.at[SECTIONS - k], along_x(k))
            copy.start()
            parts.append(copy)
        else:
            acc_f[...] = total
        kw = jnp.dot(ft_ref[k], gk[k], preferred_element_type=F32)
        vw = jnp.dot(ft_ref[k], gv[k], preferred_element_type=F32)
        if begin:
            acc_k[...] = kw
            acc_v[...] = vw
        elif k:
            acc_k[...] += kw
            acc_v[...] += vw
        else:
            kgrad_ref[...] = (acc_k[...] + kw).astype(BF16)
            vgrad_ref[...] = (acc_v[...] + vw).astype(BF16)

    order = (2, 1, 3, 0)
    n = len(order)
    first(order[0])
    first(order[1])
    second(order[0])
    for i in range(n):
        if i + 2 < n:
            first(order[i + 2])
        if i + 1 < n:
            second(order[i + 1])
        third(order[i], i == 0)
    for copy in parts:
        copy.wait_recv()
    total = acc_f[...]
    for k in (1, 2, 3):
        total = total + fr[k].astype(F32)
    fgrad_ref[...] = total.astype(BF16)
    for copy in list(near.values()) + list(seen.values()) + parts:
        copy.wait_send()


def spread(dk, dv, ft, wk, wv):
    dma = pltpu.SemaphoreType.DMA
    return pl.pallas_call(
        spread_kernel,
        out_shape=(
            jax.ShapeDtypeStruct((TILE, DEPTH), BF16),
            jax.ShapeDtypeStruct((DEPTH, GROUP * HD), BF16),
            jax.ShapeDtypeStruct((DEPTH, GROUP * HD), BF16),
        ),
        in_specs=[pl.BlockSpec(memory_space=pltpu.VMEM)] * 5,
        out_specs=(pl.BlockSpec(memory_space=pltpu.VMEM),) * 3,
        scratch_shapes=[
            pltpu.VMEM((4, TILE, GROUP * HD), BF16),
            pltpu.VMEM((4, TILE, GROUP * HD), BF16),
            pltpu.VMEM((4, TILE, DEPTH), BF16),
            pltpu.VMEM((4, TILE, DEPTH), BF16),
            pltpu.VMEM((TILE, DEPTH), F32),
            pltpu.VMEM((DEPTH, GROUP * HD), F32),
            pltpu.VMEM((DEPTH, GROUP * HD), F32),
            dma((4, 2)),
            dma((4, 4)), dma((4, 4)), dma((4, 4)), dma((4, 4)),
            dma((4, 4)), dma((4, 4)), dma((4, 4)), dma((4, 4)),
            dma((4, 2)), dma((4, 2)),
            dma((4,)), dma((4,)),
        ],
        compiler_params=pltpu.CompilerParams(
            collective_id=2, has_side_effects=True, vmem_limit_bytes=VMEM_LIMIT
        ),
        name="spread",
    )(dk, dv, ft, wk, wv)


def per_device(features, key_weight, value_weight, queries, out_grad, tile_count, tile_last):
    wk, wv = key_weight[0], value_weight[0]
    keys, values, ft = project(features, wk, wv)
    s = lax.axis_index("section")
    tiles = lax.rem(s + jnp.arange(4, dtype=jnp.int32), SECTIONS)
    counts = tile_count[tiles]
    slot = jnp.arange(TILE, dtype=jnp.int32)
    lim = jnp.where(slot[None, :] < counts[:, None], tiles[:, None], SECTIONS).reshape(4 * TILE, 1)
    out, dk, dv = attend(
        queries[0], out_grad[0], keys.reshape(4 * TILE, HD), values.reshape(4 * TILE, HD),
        lim, tile_last.reshape(1, SEQ),
    )
    fgrad, kgrad, vgrad = spread(
        dk.reshape(4, TILE, HD), dv.reshape(4, TILE, HD), ft, wk, wv
    )
    return (out[None], fgrad, kgrad[None], vgrad[None])


def solution(mesh):
    in_specs = (
        P(("dp", "section"), "tensor"),
        P("section", "tensor", None),
        P("section", "tensor", None),
        P("section", "dp", "tensor"),
        P("section", "dp", "tensor"),
        P("dp"),
        P("dp"),
    )
    out_specs = (
        P("section", "dp", "tensor"),
        P(("dp", "section"), "tensor"),
        P("section", "tensor", "dp"),
        P("section", "tensor", "dp"),
    )
    return jax.shard_map(
        per_device, mesh=mesh, in_specs=in_specs, out_specs=out_specs, check_vma=False
    )
```

```python
import functools

import jax
import jax.numpy as jnp
from jax import lax
from jax.experimental import pallas as pl
from jax.experimental.pallas import tpu as pltpu
from jax.sharding import PartitionSpec as P

MESH = pl.DeviceIdType.MESH
F32 = jnp.float32
BF16 = jnp.bfloat16
I16 = jnp.int16
HD = 128
GROUP = 8
SECTIONS = 4
RING = 4
TILE = 192
HALF = TILE // 2
DEPTH = 1024
SEQ = 256
LEVELS = 32700.0
FLOOR = -1e30
VMEM_LIMIT = 56 * 2**20


def place():
    t = lax.axis_index("tensor")
    return lax.axis_index("section"), lax.axis_index("dp"), t // 2, lax.rem(t, 2)


def along_x(d):
    s, dp, y, z = place()
    return (lax.rem(s + d, SECTIONS), dp, y * 2 + z)


def along_y(d):
    s, dp, y, z = place()
    return (s, dp, lax.rem(y + d, RING) * 2 + z)


def along_z():
    s, dp, y, z = place()
    return (s, dp, y * 2 + (1 - z))


def meet():
    barrier = pltpu.get_barrier_semaphore()
    peers = [along_x(d) for d in (1, 2, 3)] + [along_y(d) for d in (1, 2, 3)] + [along_z()]
    for peer in peers:
        pl.semaphore_signal(barrier, inc=1, device_id=peer, device_id_type=MESH)
    pl.semaphore_wait(barrier, len(peers))


def remote(src, dst, send_sem, recv_sem, device):
    return pltpu.make_async_remote_copy(
        src_ref=src, dst_ref=dst, send_sem=send_sem, recv_sem=recv_sem,
        device_id=device, device_id_type=MESH,
    )


def encode(x):
    top = jnp.maximum(jnp.max(jnp.abs(x), axis=0, keepdims=True), 1e-30)
    power = jnp.ceil(jnp.log(top) * 1.4426950408889634 + 0.0005)
    code = jnp.round(x * (jnp.exp2(-power) * LEVELS)).astype(jnp.int32).astype(I16)
    return code, power


def marks(powers):
    row = lax.broadcasted_iota(jnp.int32, (16, HD), 0)
    mark = jnp.broadcast_to(powers[0], (16, HD))
    for i, power in enumerate(powers[1:]):
        mark = jnp.where(row == i + 1, power, mark)
    return mark.astype(jnp.int32).astype(I16)


def units(mark):
    return jnp.exp2(mark.astype(jnp.int32).astype(F32)) * (1.0 / LEVELS)


def as_f32(code):
    return code.astype(jnp.int32).astype(F32)


ACROSS = (((1,), (1,)), ((), ()))
CHUNKS = ((0, 0), (0, 1), (1, 0), (3, 0), (1, 1), (3, 1), (2, 0), (2, 1))
TILES = (2, 1, 3, 0)


def main_kernel(
    count_ref, last_ref, f_ref, wk_ref, wv_ref, q_ref, g_ref,
    gk_out, gv_out, ft_out, att_out, fgrad_out,
    fg, wk, wv, q, g, pk, pv, kz_out, kz_in, ky_out, ky_in, vy_out, vy_in, vz_out, vz_in, sv,
    keys, values, expo, dprobs, tops, sums, dots, probs, dscores, dks, dvs, gk, gv, fs, fr, acc,
    ft, att, fgrad,
    load, store, own, x_send, x_recv, kz_send, kz_recv, ky_send, ky_recv,
    vy_send, vy_recv, vz_send, vz_recv,
    az_s, az_r, as_s, as_r, a2_s, a2_r, by_s, by_r, b2_s, b2_r, bz_s, bz_r, fx_s, fx_r,
):
    s, dp, y, z = place()
    scale = HD ** -0.5
    loads = [
        pltpu.make_async_copy(src, dst, load.at[i])
        for i, (src, dst) in enumerate(
            ((f_ref, fg.at[0]), (wv_ref, wv), (wk_ref, wk), (q_ref, q), (g_ref, g))
        )
    ]
    for copy in loads:
        copy.start()
    meet()
    sends = []

    def go(*args):
        copy = remote(*args)
        copy.start()
        sends.append(copy)
        return copy

    def half(k, h):
        return fg.at[k, pl.ds(h * HALF, HALF)]

    loads[0].wait()
    gathers = {}
    for h in range(2):
        for d in (1, 3):
            k = SECTIONS - d
            gathers[k, h] = go(half(0, h), half(k, h), x_send.at[k, h], x_recv.at[k, h], along_x(d))

    first_k, first_v, second_k, second_v = {}, {}, {}, {}

    def head_at(d, r):
        return lax.rem(y + d, RING) * 2 + lax.rem(z + r, 2)

    def start(i):
        k, h = CHUNKS[i]
        if k:
            gathers[k, h].wait_recv()
        if (k, h) == (1, 0):
            gathers[2, 0] = go(half(1, 0), half(2, 0), x_send.at[2, 0], x_recv.at[2, 0], along_x(3))
        if (k, h) == (3, 1):
            gathers[2, 1] = go(half(3, 1), half(2, 1), x_send.at[2, 1], x_recv.at[2, 1], along_x(1))
        if i == 0:
            loads[1].wait()
        rows = fg[k, h * HALF:(h + 1) * HALF, :]
        v = jnp.dot(rows, wv[...], preferred_element_type=F32)
        for head in range(8):
            pv[i, head] = v[:, head * HD:(head + 1) * HD]
        for d in (2, 1, 3):
            for r in range(2):
                vy_out[i, d, r] = pv[i, head_at(d, r)].astype(BF16)
            first_v[i, d] = go(
                vy_out.at[i, d], vy_in.at[i, RING - d],
                vy_send.at[i, d], vy_recv.at[i, RING - d], along_y(d),
            )
        if i == 0:
            loads[2].wait()
        p = jnp.dot(rows, wk[...], preferred_element_type=F32)
        for head in range(8):
            pk[i, head] = p[:, head * HD:(head + 1) * HD]
        powers = []
        for d in range(RING):
            code, power = encode(pk[i, head_at(d, 1)])
            kz_out[i, d * HALF:(d + 1) * HALF, :] = code
            powers.append(power)
        kz_out[i, 4 * HALF:4 * HALF + 16, :] = marks(powers)
        first_k[i] = go(kz_out.at[i], kz_in.at[i], kz_send.at[i], kz_recv.at[i], along_z())

    def middle(i):
        first_k[i].wait_recv()
        unit = units(kz_in[i, 4 * HALF:4 * HALF + 16, :])
        for d in (2, 1, 3, 0):
            head = head_at(d, 0)
            total = pk[i, head] + as_f32(kz_in[i, d * HALF:(d + 1) * HALF, :]) * unit[d:d + 1]
            if d:
                code, power = encode(total)
                ky_out[i, d, 0:HALF, :] = code
                ky_out[i, d, HALF:HALF + 16, :] = marks([power])
                second_k[i, d] = go(
                    ky_out.at[i, d], ky_in.at[i, RING - d],
                    ky_send.at[i, d], ky_recv.at[i, RING - d], along_y(d),
                )
            else:
                pk[i, head] = total
        for d in (1, 3, 2):
            first_v[i, RING - d].wait_recv()
        for r in (1, 0):
            total = pv[i, head_at(0, r)]
            for d in (1, 2, 3):
                total = total + vy_in[i, d, r].astype(F32)
            if r:
                vz_out[i] = total.astype(BF16)
                second_v[i] = go(vz_out.at[i], vz_in.at[i], vz_send.at[i], vz_recv.at[i], along_z())
            else:
                sv[i] = total

    def finish(i):
        k, h = CHUNKS[i]
        spot = slice(k * TILE + h * HALF, k * TILE + (h + 1) * HALF)
        for d in (1, 3, 2):
            second_k[i, RING - d].wait_recv()
        total = pk[i, head_at(0, 0)]
        for d in (1, 2, 3):
            unit = units(ky_in[i, d, HALF:HALF + 16, :])
            total = total + as_f32(ky_in[i, d, 0:HALF, :]) * unit[0:1]
        key = total.astype(BF16)
        keys[spot, :] = key
        second_v[i].wait_recv()
        value = (sv[i] + vz_in[i].astype(F32)).astype(BF16)
        values[spot, :] = value
        tile = lax.rem(s + k, SECTIONS)
        slot = lax.broadcasted_iota(jnp.int32, (HALF, SEQ), 0) + h * HALF
        limit = jnp.where(slot < count_ref[tile], tile, SECTIONS)
        visible = limit <= last_ref[...]
        for j in range(GROUP):
            cols = slice(j * HD, (j + 1) * HD)
            wide = slice(j * SEQ, (j + 1) * SEQ)
            scores = lax.dot_general(key, q[:, cols], ACROSS, preferred_element_type=F32) * scale
            masked = jnp.where(visible, scores, -jnp.inf)
            top = jnp.maximum(jnp.max(masked, axis=0, keepdims=True), FLOOR)
            e = jnp.exp(masked - top)
            dprob = lax.dot_general(value, g[:, cols], ACROSS, preferred_element_type=F32)
            expo[spot, wide] = e
            dprobs[spot, wide] = dprob
            tops[i:i + 1, wide] = top
            sums[i:i + 1, wide] = jnp.sum(e, axis=0, keepdims=True)
            dots[i:i + 1, wide] = jnp.sum(e * dprob, axis=0, keepdims=True)

    def turn(a):
        ft[:, a * 2 * TILE:(a + 1) * 2 * TILE] = jnp.concatenate([fg[2 * a], fg[2 * a + 1]], axis=0).T
        copy = pltpu.make_async_copy(
            ft.at[:, pl.ds(a * 2 * TILE, 2 * TILE)], ft_out.at[:, pl.ds(a * 2 * TILE, 2 * TILE)],
            store.at[a],
        )
        copy.start()
        return copy

    stores = []
    n = len(CHUNKS)
    for i in range(n + 2):
        if i < n:
            start(i)
        if 0 <= i - 1 < n:
            middle(i - 1)
        if i == 2:
            loads[3].wait()
            loads[4].wait()
        if 0 <= i - 2:
            finish(i - 2)
        if i == 5:
            stores.append(turn(0))

    peak = jnp.max(tops[...], axis=0, keepdims=True)
    share = jnp.exp(tops[...] - peak)
    inverse = 1.0 / jnp.sum(share * sums[...], axis=0, keepdims=True)
    share = share * inverse
    sums[...] = share
    dots[0:1, :] = jnp.sum(share * dots[...], axis=0, keepdims=True)

    def cols(head, n=1):
        return pl.ds(pl.multiple_of(head * HD, HD), n * HD)

    mine = cols(y * 2 + z)
    owned, az, ae, a2, by, b2, bz = {}, {}, {}, {}, {}, {}, {}

    def attend(k):
        dk = dv = None
        for j in range(GROUP):
            narrow = slice(j * HD, (j + 1) * HD)
            wide = slice(j * SEQ, (j + 1) * SEQ)
            delta = dots[0:1, wide]
            for h in range(2):
                i = CHUNKS.index((k, h))
                spot = slice(k * TILE + h * HALF, k * TILE + (h + 1) * HALF)
                p = expo[spot, wide] * sums[i:i + 1, wide]
                probs[spot, wide] = p.astype(BF16)
                dscores[h * HALF:(h + 1) * HALF, wide] = (p * (dprobs[spot, wide] - delta) * scale).astype(BF16)
            whole = slice(k * TILE, (k + 1) * TILE)
            dv_j = jnp.dot(probs[whole, wide], g[:, narrow], preferred_element_type=F32)
            dk_j = jnp.dot(dscores[:, wide], q[:, narrow], preferred_element_type=F32)
            dv = dv_j if j == 0 else dv + dv_j
            dk = dk_j if j == 0 else dk + dk_j
        dvs[k] = dv.astype(BF16)
        dks[k] = dk.astype(BF16)

    def ways(k):
        return (1, 3) if TILES.index(k) % 2 == 0 else (3, 1)

    def zero(k):
        attend(k)
        by[k, 3] = go(dvs.at[k], gv.at[k, :, mine], by_s.at[k, 1], by_r.at[k, 3], along_y(1))
        by[k, 1] = go(dvs.at[k], gv.at[k, :, mine], by_s.at[k, 3], by_r.at[k, 1], along_y(3))
        az[k] = go(dks.at[k], gk.at[k, :, mine], az_s.at[k], az_r.at[k], along_z())
        bz[k, 0] = go(dvs.at[k], gv.at[k, :, mine], bz_s.at[k, 0], bz_r.at[k, 0], along_z())
        for j, (src, dst) in enumerate(((dks, gk), (dvs, gv))):
            copy = pltpu.make_async_copy(src.at[k], dst.at[k, :, mine], own.at[k, j])
            copy.start()
            owned[k, j] = copy

    def one(k):
        ahead, behind = ways(k)
        owned[k, 0].wait()
        az[k].wait_recv()
        pair = cols(y * 2, 2)
        for d in (1, 3):
            ae[k, RING - d] = go(
                gk.at[k, :, pair], gk.at[k, :, pair],
                as_s.at[k, d], as_r.at[k, RING - d], along_y(d),
            )
        for d in (behind, ahead):
            by[k, d].wait_recv()
            head = cols(head_at(d, 0))
            if d == behind:
                b2[k] = go(gv.at[k, :, head], gv.at[k, :, head], b2_s.at[k], b2_r.at[k], along_y(ahead))
            bz[k, d] = go(gv.at[k, :, head], gv.at[k, :, head], bz_s.at[k, d], bz_r.at[k, d], along_z())

    def two(k):
        ahead, behind = ways(k)
        ae[k, behind].wait_recv()
        pair = cols(lax.rem(y + behind, RING) * 2, 2)
        a2[k] = go(gk.at[k, :, pair], gk.at[k, :, pair], a2_s.at[k], a2_r.at[k], along_y(ahead))
        b2[k].wait_recv()
        head = cols(head_at(2, 0))
        bz[k, 2] = go(gv.at[k, :, head], gv.at[k, :, head], bz_s.at[k, 2], bz_r.at[k, 2], along_z())

    parts = []

    def three(k):
        ahead, behind = ways(k)
        owned[k, 1].wait()
        ae[k, ahead].wait_recv()
        a2[k].wait_recv()
        for d in range(RING):
            bz[k, d].wait_recv()
        for j, (src, dst) in enumerate(((gk, gk_out), (gv, gv_out))):
            copy = pltpu.make_async_copy(src.at[k], dst.at[k], store.at[2 + 2 * k + j])
            copy.start()
            stores.append(copy)
        total = lax.dot_general(gk[k], wk[...], ACROSS, preferred_element_type=F32)
        total += lax.dot_general(gv[k], wv[...], ACROSS, preferred_element_type=F32)
        if k:
            fs[k] = total.astype(BF16)
            parts.append(
                go(fs.at[k], fr.at[SECTIONS - k], fx_s.at[k], fx_r.at[SECTIONS - k], along_x(k))
            )
        else:
            acc[...] = total

    def forward():
        turned = values[...].T
        for j in range(GROUP):
            out = jnp.dot(turned, probs[:, j * SEQ:(j + 1) * SEQ], preferred_element_type=F32)
            att[:, j * HD:(j + 1) * HD] = out.T.astype(BF16)
        copy = pltpu.make_async_copy(att, att_out, store.at[10])
        copy.start()
        stores.append(copy)

    n = len(TILES)
    for i in range(n + 3):
        if i < n:
            zero(TILES[i])
        if 0 <= i - 1 < n:
            one(TILES[i - 1])
        if i == n - 1:
            stores.append(turn(1))
        if i == n:
            forward()
        if 0 <= i - 2 < n:
            two(TILES[i - 2])
        if 0 <= i - 3:
            three(TILES[i - 3])
    for copy in parts:
        copy.wait_recv()
    total = acc[...]
    for k in (1, 2, 3):
        total = total + fr[k].astype(F32)
    fgrad[...] = total.astype(BF16)
    copy = pltpu.make_async_copy(fgrad, fgrad_out, store.at[11])
    copy.start()
    stores.append(copy)
    for copy in sends:
        copy.wait_send()
    for copy in stores:
        copy.wait()


def main(count, last, f, wk, wv, q, g):
    dma = pltpu.SemaphoreType.DMA
    vmem = pltpu.VMEM
    anywhere = pl.BlockSpec(memory_space=pl.ANY)
    rows = 4 * TILE
    wide = GROUP * SEQ
    return pl.pallas_call(
        main_kernel,
        out_shape=(
            jax.ShapeDtypeStruct((4, TILE, GROUP * HD), BF16),
            jax.ShapeDtypeStruct((4, TILE, GROUP * HD), BF16),
            jax.ShapeDtypeStruct((DEPTH, rows), BF16),
            jax.ShapeDtypeStruct((SEQ, GROUP * HD), BF16),
            jax.ShapeDtypeStruct((TILE, DEPTH), BF16),
        ),
        in_specs=[
            pl.BlockSpec(memory_space=pltpu.SMEM), pl.BlockSpec(memory_space=pltpu.VMEM),
        ] + [anywhere] * 5,
        out_specs=(anywhere,) * 5,
        scratch_shapes=[
            vmem((4, TILE, DEPTH), BF16),
            vmem((DEPTH, GROUP * HD), BF16),
            vmem((DEPTH, GROUP * HD), BF16),
            vmem((SEQ, GROUP * HD), BF16),
            vmem((SEQ, GROUP * HD), BF16),
            vmem((8, 8, HALF, HD), F32),
            vmem((8, 8, HALF, HD), F32),
            vmem((8, 4 * HALF + 16, HD), I16),
            vmem((8, 4 * HALF + 16, HD), I16),
            vmem((8, 4, HALF + 16, HD), I16),
            vmem((8, 4, HALF + 16, HD), I16),
            vmem((8, 4, 2, HALF, HD), BF16),
            vmem((8, 4, 2, HALF, HD), BF16),
            vmem((8, HALF, HD), BF16),
            vmem((8, HALF, HD), BF16),
            vmem((8, HALF, HD), F32),
            vmem((rows, HD), BF16),
            vmem((rows, HD), BF16),
            vmem((rows, wide), F32),
            vmem((rows, wide), F32),
            vmem((8, wide), F32),
            vmem((8, wide), F32),
            vmem((8, wide), F32),
            vmem((rows, wide), BF16),
            vmem((TILE, wide), BF16),
            vmem((4, TILE, HD), BF16),
            vmem((4, TILE, HD), BF16),
            vmem((4, TILE, GROUP * HD), BF16),
            vmem((4, TILE, GROUP * HD), BF16),
            vmem((4, TILE, DEPTH), BF16),
            vmem((4, TILE, DEPTH), BF16),
            vmem((TILE, DEPTH), F32),
            vmem((DEPTH, rows), BF16),
            vmem((SEQ, GROUP * HD), BF16),
            vmem((TILE, DEPTH), BF16),
            dma((5,)), dma((12,)), dma((4, 2)),
            dma((4, 2)), dma((4, 2)),
            dma((8,)), dma((8,)),
            dma((8, 4)), dma((8, 4)),
            dma((8, 4)), dma((8, 4)),
            dma((8,)), dma((8,)),
            dma((4,)), dma((4,)),
            dma((4, 4)), dma((4, 4)),
            dma((4,)), dma((4,)),
            dma((4, 4)), dma((4, 4)),
            dma((4,)), dma((4,)),
            dma((4, 4)), dma((4, 4)),
            dma((4,)), dma((4,)),
        ],
        compiler_params=pltpu.CompilerParams(
            collective_id=1, has_side_effects=True, vmem_limit_bytes=VMEM_LIMIT
        ),
        name="main",
    )(count, last, f, wk, wv, q, g)


def close_kernel(ft_ref, gk_ref, gv_ref, att_ref, fgrad_ref, kw_ref, vw_ref, att_out, fgrad_out):
    turned = ft_ref[...]
    kw_ref[...] = jnp.dot(turned, gk_ref[...], preferred_element_type=F32).astype(BF16)
    vw_ref[...] = jnp.dot(turned, gv_ref[...], preferred_element_type=F32).astype(BF16)
    att_out[...] = att_ref[...]
    fgrad_out[...] = fgrad_ref[...]


def close(ft, gk, gv, att, fgrad):
    step = 256

    def block(rows):
        return pl.BlockSpec((rows, step), lambda i: (0, i))

    rows = 4 * TILE
    return pl.pallas_call(
        close_kernel,
        grid=(DEPTH // step,),
        out_shape=(
            jax.ShapeDtypeStruct((DEPTH, GROUP * HD), BF16),
            jax.ShapeDtypeStruct((DEPTH, GROUP * HD), BF16),
            jax.ShapeDtypeStruct((SEQ, GROUP * HD), BF16),
            jax.ShapeDtypeStruct((TILE, DEPTH), BF16),
        ),
        in_specs=[
            pl.BlockSpec((DEPTH, rows), lambda i: (0, 0)),
            block(rows), block(rows), block(SEQ), block(TILE),
        ],
        out_specs=(block(DEPTH), block(DEPTH), block(SEQ), block(TILE)),
        compiler_params=pltpu.CompilerParams(vmem_limit_bytes=VMEM_LIMIT),
        name="close",
    )(ft, gk, gv, att, fgrad)


def per_device(features, key_weight, value_weight, queries, out_grad, tile_count, tile_last):
    gk, gv, ft, att, fgrad = main(
        tile_count, tile_last.reshape(1, SEQ), features,
        key_weight[0], value_weight[0], queries[0], out_grad[0],
    )
    rows = 4 * TILE
    kgrad, vgrad, out, fgrad = close(
        ft, gk.reshape(rows, GROUP * HD), gv.reshape(rows, GROUP * HD), att, fgrad
    )
    return (out[None], fgrad, kgrad[None], vgrad[None])


def solution(mesh):
    in_specs = (
        P(("dp", "section"), "tensor"),
        P("section", "tensor", None),
        P("section", "tensor", None),
        P("section", "dp", "tensor"),
        P("section", "dp", "tensor"),
        P("dp"),
        P("dp"),
    )
    out_specs = (
        P("section", "dp", "tensor"),
        P(("dp", "section"), "tensor"),
        P("section", "tensor", "dp"),
        P("section", "tensor", "dp"),
    )
    return jax.shard_map(
        per_device, mesh=mesh, in_specs=in_specs, out_specs=out_specs, check_vma=False
    )
```

```python
import functools

import jax
import jax.numpy as jnp
from jax import lax
from jax.experimental import pallas as pl
from jax.experimental.pallas import tpu as pltpu
from jax.sharding import PartitionSpec as P

MESH = pl.DeviceIdType.MESH
F32 = jnp.float32
BF16 = jnp.bfloat16
I16 = jnp.int16
HD = 128
GROUP = 8
SECTIONS = 4
RING = 4
TILE = 192
HALF = TILE // 2
DEPTH = 1024
SEQ = 256
LEVELS = 32700.0
FLOOR = -1e30
VMEM_LIMIT = 58 * 2**20


def place():
    t = lax.axis_index("tensor")
    return lax.axis_index("section"), lax.axis_index("dp"), t // 2, lax.rem(t, 2)


def along_x(d):
    s, dp, y, z = place()
    return (lax.rem(s + d, SECTIONS), dp, y * 2 + z)


def along_y(d):
    s, dp, y, z = place()
    return (s, dp, lax.rem(y + d, RING) * 2 + z)


def along_z():
    s, dp, y, z = place()
    return (s, dp, y * 2 + (1 - z))


def greet():
    barrier = pltpu.get_barrier_semaphore()
    peers = [along_x(d) for d in (1, 3)] + [along_y(d) for d in (1, 2, 3)] + [along_z()]
    for peer in peers:
        pl.semaphore_signal(barrier, inc=1, device_id=peer, device_id_type=MESH)
    return barrier, len(peers)


def remote(src, dst, send_sem, recv_sem, device):
    return pltpu.make_async_remote_copy(
        src_ref=src, dst_ref=dst, send_sem=send_sem, recv_sem=recv_sem,
        device_id=device, device_id_type=MESH,
    )


def encode(x):
    top = jnp.maximum(jnp.max(jnp.abs(x), axis=0, keepdims=True), 1e-30)
    power = jnp.ceil(jnp.log(top) * 1.4426950408889634 + 0.0005)
    code = jnp.round(x * (jnp.exp2(-power) * LEVELS)).astype(jnp.int32).astype(I16)
    return code, power


def marks(powers):
    row = lax.broadcasted_iota(jnp.int32, (16, HD), 0)
    mark = jnp.broadcast_to(powers[0], (16, HD))
    for i, power in enumerate(powers[1:]):
        mark = jnp.where(row == i + 1, power, mark)
    return mark.astype(jnp.int32).astype(I16)


def units(mark):
    return jnp.exp2(mark.astype(jnp.int32).astype(F32)) * (1.0 / LEVELS)


def as_f32(code):
    return code.astype(jnp.int32).astype(F32)


ACROSS = (((1,), (1,)), ((), ()))
CHUNKS = ((0, 0), (0, 1), (1, 0), (3, 0), (1, 1), (3, 1), (2, 0), (2, 1))
UNITS = (((2, 0), (2, 1)), ((1, 0), (3, 0)), ((1, 1), (3, 1)), ((0, 0), (0, 1)))
ROWS = sum(UNITS, ())
RELAYED = 6
SLOT = {1: 0, 3: 1, 2: 2}


def ahead_of(i):
    return 1 if i % 2 == 0 else 3


def main_kernel(
    count_hbm, last_hbm, f_ref, wk_ref, wv_ref, q_ref, g_ref,
    kgrad, vgrad, att, fgrad,
    fg, wk, wv, q, g, pk, pv, kz_out, kz_in, ky_out, ky_in, vy_out, vy_in, vz_out, vz_in, sv,
    keys, values, expo, dprobs, tops, sums, dots, probs, dscores, dks, dvs, gk, gv, fs, fr, acc,
    ft, count, last,
    load, out1, out3, x_out, x_in, kz_sem, v1_sem, v2_sem, k1_sem, k2_sem, vz_sem,
    a1_sem, a2_sem, a3_sem, over_sem, part_sem,
):
    s, dp, y, z = place()
    scale = HD ** -0.5
    loads = [
        pltpu.make_async_copy(src, dst, load.at[i])
        for i, (src, dst) in enumerate((
            (f_ref, fg.at[0]), (wv_ref, wv), (wk_ref, wk), (q_ref, q), (g_ref, g),
            (last_hbm, last), (count_hbm, count),
        ))
    ]
    for copy in loads:
        copy.start()
    barrier, peers = greet()

    def go(*args):
        remote(*args).start()

    def done(ref, sem):
        pltpu.make_async_copy(ref, ref, sem).wait()

    def half(k, h):
        return fg.at[k, pl.ds(h * HALF, HALF)]

    def pass_x(k, h, to, d, sem):
        go(half(k, h), half(to, h), sem, x_in.at[to - 1, h], along_x(d))

    def head_at(d, r):
        return lax.rem(y + d, RING) * 2 + lax.rem(z + r, 2)

    def compute_v(i):
        k, h = CHUNKS[i]
        v = jnp.dot(fg[k, h * HALF:(h + 1) * HALF, :], wv[...], preferred_element_type=F32)
        for head in range(8):
            pv[i, head] = v[:, head * HD:(head + 1) * HD]
        for d in (2, RING - ahead_of(i)) if i < RELAYED else (2, 1, 3):
            for r in range(2):
                vy_out[i, SLOT[d], r] = pv[i, head_at(d, r)].astype(BF16)

    def compute_k(i):
        k, h = CHUNKS[i]
        p = jnp.dot(fg[k, h * HALF:(h + 1) * HALF, :], wk[...], preferred_element_type=F32)
        for head in range(8):
            pk[i, head] = p[:, head * HD:(head + 1) * HD]
        powers = []
        for d in range(RING):
            code, power = encode(pk[i, head_at(d, 1)])
            kz_out[i, d * HALF:(d + 1) * HALF, :] = code
            powers.append(power)
        kz_out[i, 4 * HALF:4 * HALF + 16, :] = marks(powers)

    def send_y(i, d, to, at, sem):
        go(vy_out.at[i, SLOT[d]], vy_in.at[i, SLOT[at]], out1, sem.at[i], along_y(to))

    def send_v(i):
        ahead = ahead_of(i)
        if i < RELAYED:
            send_y(i, 2, ahead, 2, v1_sem)
            send_y(i, RING - ahead, RING - ahead, ahead, v2_sem)
        else:
            for d in (2, 1, 3):
                send_y(i, d, d, RING - d, v1_sem)

    def send_z(i):
        go(kz_out.at[i], kz_in.at[i], out1, kz_sem.at[i], along_z())

    def start(i):
        k, h = CHUNKS[i]
        if k == 2:
            done(half(k, h), x_in.at[k - 1, h])
        compute_v(i)
        send_v(i)
        compute_k(i)
        send_z(i)

    def send_k(i, d, to, at, total, sem):
        code, power = encode(total)
        ky_out[i, SLOT[d], 0:HALF, :] = code
        ky_out[i, SLOT[d], HALF:HALF + 16, :] = marks([power])
        go(ky_out.at[i, SLOT[d]], ky_in.at[i, SLOT[at]], out1, sem.at[i], along_y(to))

    def got_k(i, at):
        unit = units(ky_in[i, at, HALF:HALF + 16, :])
        return as_f32(ky_in[i, at, 0:HALF, :]) * unit[0:1]

    def gather_v(i, n, sem):
        done(vy_in.at[i, pl.ds(0, n)], sem.at[i])
        for r in (1, 0):
            total = pv[i, head_at(0, r)]
            for at in range(n):
                total = total + vy_in[i, at, r].astype(F32)
            if r:
                vz_out[i] = total.astype(BF16)
                go(vz_out.at[i], vz_in.at[i], out1, vz_sem.at[i], along_z())
            else:
                sv[i] = total

    def middle(i):
        ahead = ahead_of(i)
        behind = RING - ahead
        if i < RELAYED:
            done(vy_in.at[i, 2], v1_sem.at[i])
            for r in range(2):
                total = pv[i, head_at(ahead, r)] + vy_in[i, 2, r].astype(F32)
                vy_out[i, SLOT[ahead], r] = total.astype(BF16)
            send_y(i, ahead, ahead, behind, v2_sem)
        done(kz_in.at[i], kz_sem.at[i])
        unit = units(kz_in[i, 4 * HALF:4 * HALF + 16, :])
        for d in (2, 1, 3, 0):
            head = head_at(d, 0)
            total = pk[i, head] + as_f32(kz_in[i, d * HALF:(d + 1) * HALF, :]) * unit[d:d + 1]
            if i >= RELAYED and d:
                send_k(i, d, d, RING - d, total, k2_sem)
            elif d == 2:
                send_k(i, 2, behind, 2, total, k1_sem)
            elif d == ahead:
                send_k(i, ahead, ahead, behind, total, k2_sem)
            else:
                pk[i, head] = total
        if i >= RELAYED:
            gather_v(i, 3, v1_sem)

    def relay(i):
        ahead = ahead_of(i)
        behind = RING - ahead
        done(ky_in.at[i, 2], k1_sem.at[i])
        send_k(i, behind, behind, ahead, pk[i, head_at(behind, 0)] + got_k(i, 2), k2_sem)
        gather_v(i, 2, v2_sem)

    def finish(i):
        k, h = CHUNKS[i]
        at = ROWS.index((k, h)) * HALF
        spot = slice(at, at + HALF)
        n = 2 if i < RELAYED else 3
        done(ky_in.at[i, pl.ds(0, n)], k2_sem.at[i])
        total = pk[i, head_at(0, 0)]
        for at in range(n):
            total = total + got_k(i, at)
        key = total.astype(BF16)
        keys[spot, :] = key
        done(vz_in.at[i], vz_sem.at[i])
        value = (sv[i] + vz_in[i].astype(F32)).astype(BF16)
        values[spot, :] = value
        tile = lax.rem(s + k, SECTIONS)
        slot = lax.broadcasted_iota(jnp.int32, (HALF, SEQ), 0) + h * HALF
        limit = jnp.where(slot < count[tile], tile, SECTIONS)
        visible = limit <= last[...]
        for j in range(GROUP):
            cols = slice(j * HD, (j + 1) * HD)
            wide = slice(j * SEQ, (j + 1) * SEQ)
            scores = lax.dot_general(key, q[:, cols], ACROSS, preferred_element_type=F32) * scale
            masked = jnp.where(visible, scores, -jnp.inf)
            top = jnp.maximum(jnp.max(masked, axis=0, keepdims=True), FLOOR)
            e = jnp.exp(masked - top)
            dprob = lax.dot_general(value, g[:, cols], ACROSS, preferred_element_type=F32)
            expo[spot, wide] = e
            dprobs[spot, wide] = dprob
            tops[i:i + 1, wide] = top
            sums[i:i + 1, wide] = jnp.sum(e, axis=0, keepdims=True)
            dots[i:i + 1, wide] = jnp.sum(e * dprob, axis=0, keepdims=True)

    def turn(a):
        rows = [fg[k, h * HALF:(h + 1) * HALF, :] for k, h in ROWS[4 * a:4 * a + 4]]
        ft[:, a * 2 * TILE:(a + 1) * 2 * TILE] = jnp.concatenate(rows, axis=0).T

    loads[0].wait()
    loads[1].wait()
    compute_v(0)
    pl.semaphore_wait(barrier, peers)
    pass_x(0, 0, 3, 1, x_out)
    pass_x(0, 0, 1, 3, x_out)
    send_v(0)
    loads[2].wait()
    compute_k(0)
    send_z(0)
    start(1)
    middle(0)
    done(fg.at[0], x_out)
    pass_x(0, 1, 3, 1, out1)
    pass_x(0, 1, 1, 3, out1)
    middle(1)
    done(half(1, 0), x_in.at[0, 0])
    pass_x(1, 0, 2, 3, out1)
    start(2)
    done(half(3, 0), x_in.at[2, 0])
    start(3)
    for copy in loads[3:]:
        copy.wait()
    relay(0)
    relay(1)
    done(half(3, 1), x_in.at[2, 1])
    pass_x(3, 1, 2, 1, out1)
    done(half(1, 1), x_in.at[0, 1])
    start(4)
    middle(2)
    finish(0)
    start(5)
    middle(3)
    finish(1)
    relay(2)
    start(6)
    middle(4)
    relay(3)
    finish(2)
    start(7)
    middle(5)
    relay(4)
    finish(3)
    middle(6)
    relay(5)
    finish(4)
    turn(0)
    turn(1)
    middle(7)
    finish(5)
    finish(6)
    finish(7)

    peak = jnp.max(tops[...], axis=0, keepdims=True)
    share = jnp.exp(tops[...] - peak)
    inverse = 1.0 / jnp.sum(share * sums[...], axis=0, keepdims=True)
    share = share * inverse
    sums[...] = share
    dots[0:1, :] = jnp.sum(share * dots[...], axis=0, keepdims=True)

    def cols(head, n=1):
        return pl.ds(pl.multiple_of(head * HD, HD), n * HD)

    mine = cols(y * 2 + z)

    def attend(k):
        dk = dv = None
        for j in range(GROUP):
            narrow = slice(j * HD, (j + 1) * HD)
            wide = slice(j * SEQ, (j + 1) * SEQ)
            delta = dots[0:1, wide]
            for h in range(2):
                i = CHUNKS.index(UNITS[k][h])
                spot = slice(k * TILE + h * HALF, k * TILE + (h + 1) * HALF)
                p = expo[spot, wide] * sums[i:i + 1, wide]
                probs[spot, wide] = p.astype(BF16)
                dscores[h * HALF:(h + 1) * HALF, wide] = (p * (dprobs[spot, wide] - delta) * scale).astype(BF16)
            whole = slice(k * TILE, (k + 1) * TILE)
            dv_j = jnp.dot(probs[whole, wide], g[:, narrow], preferred_element_type=F32)
            dk_j = jnp.dot(dscores[:, wide], q[:, narrow], preferred_element_type=F32)
            dv = dv_j if j == 0 else dv + dv_j
            dk = dk_j if j == 0 else dk + dk_j
        for ref, into, value in ((dvs, gv, dv), (dks, gk, dk)):
            rounded = value.astype(BF16)
            ref[k] = rounded
            into[k, :, mine] = rounded

    def ways(k):
        return (1, 3) if k % 2 == 0 else (3, 1)

    def zero(k):
        go(dvs.at[k], gv.at[k, :, mine], out3, a1_sem.at[k], along_y(1))
        go(dvs.at[k], gv.at[k, :, mine], out3, a1_sem.at[k], along_y(3))
        go(dks.at[k], gk.at[k, :, mine], out3, a1_sem.at[k], along_z())
        go(dvs.at[k], gv.at[k, :, mine], out3, a3_sem.at[k], along_z())

    def one(k):
        ahead, behind = ways(k)
        done(gk.at[k, :, pl.ds(0, 3 * HD)], a1_sem.at[k])
        pair = cols(y * 2, 2)
        go(gk.at[k, :, pair], gk.at[k, :, pair], out3, a2_sem.at[k], along_y(ahead))
        head = cols(head_at(behind, 0))
        go(gv.at[k, :, head], gv.at[k, :, head], out3, a2_sem.at[k], along_y(ahead))
        go(gk.at[k, :, pair], gk.at[k, :, pair], out3, a3_sem.at[k], along_y(behind))
        for d in (behind, ahead):
            head = cols(head_at(d, 0))
            go(gv.at[k, :, head], gv.at[k, :, head], out3, a3_sem.at[k], along_z())

    def two(k):
        ahead, behind = ways(k)
        done(gk.at[k, :, pl.ds(0, 3 * HD)], a2_sem.at[k])
        pair = cols(lax.rem(y + behind, RING) * 2, 2)
        go(gk.at[k, :, pair], gk.at[k, :, pair], out3, a3_sem.at[k], along_y(ahead))
        head = cols(head_at(2, 0))
        go(gv.at[k, :, head], gv.at[k, :, head], out3, a3_sem.at[k], along_z())

    def three(k):
        done(gk.at[k], a3_sem.at[k])
        total = lax.dot_general(gk[k], wk[...], ACROSS, preferred_element_type=F32)
        total += lax.dot_general(gv[k], wv[...], ACROSS, preferred_element_type=F32)
        for h, (tile, part) in enumerate(UNITS[k]):
            half_total = total[h * HALF:(h + 1) * HALF]
            if tile == 0:
                acc[h * HALF:(h + 1) * HALF, :] = half_total
                continue
            way = tile if tile != 2 else (3, 1)[part]
            if (tile, part) in ((1, 1), (3, 0)):
                done(fr.at[2, part], over_sem.at[part])
                half_total = half_total + fr[2, part].astype(F32)
            fs[tile, part] = half_total.astype(BF16)
            if tile == 2:
                go(fs.at[tile, part], fr.at[2, part], out3, over_sem.at[part], along_x(way))
            else:
                go(fs.at[tile, part], fr.at[SLOT[SECTIONS - way], part], out3, part_sem, along_x(way))

    def weights(a, j):
        rows = slice(a * 2 * TILE, (a + 1) * 2 * TILE)
        side = slice(j * DEPTH, (j + 1) * DEPTH)
        src, dst = ((gk, kgrad), (gv, vgrad))[j]
        rhs = jnp.concatenate([src[2 * a], src[2 * a + 1]], axis=0)
        total = jnp.dot(ft[:, rows], rhs, preferred_element_type=F32)
        if a == 0:
            expo[0:3 * SEQ, side] = total[0:3 * SEQ]
            dprobs[0:SEQ, side] = total[3 * SEQ:4 * SEQ]
        else:
            dst[0:3 * SEQ, :] = (expo[0:3 * SEQ, side] + total[0:3 * SEQ]).astype(BF16)
            dst[3 * SEQ:4 * SEQ, :] = (dprobs[0:SEQ, side] + total[3 * SEQ:4 * SEQ]).astype(BF16)

    def forward():
        turned = values[...].T
        for j in range(GROUP):
            out = jnp.dot(turned, probs[:, j * SEQ:(j + 1) * SEQ], preferred_element_type=F32)
            att[:, j * HD:(j + 1) * HD] = out.T.astype(BF16)

    attend(0)
    zero(0)
    attend(1)
    zero(1)
    one(0)
    attend(2)
    zero(2)
    one(1)
    two(0)
    attend(3)
    zero(3)
    one(2)
    two(1)
    three(0)
    one(3)
    forward()
    two(2)
    three(1)
    two(3)
    weights(0, 0)
    three(2)
    weights(0, 1)
    three(3)
    weights(1, 0)
    weights(1, 1)
    done(fr.at[pl.ds(0, 2)], part_sem)
    for h in range(2):
        rows = slice(h * HALF, (h + 1) * HALF)
        total = acc[rows, :]
        for at in (0, 1):
            total = total + fr[at, h].astype(F32)
        fgrad[rows, :] = total.astype(BF16)
    done(expo.at[pl.ds(0, 448)], out1)
    done(expo.at[pl.ds(0, 480)], out3)


def main(count, last, f, wk, wv, q, g):
    dma = pltpu.SemaphoreType.DMA
    vmem = pltpu.VMEM
    held = pl.BlockSpec(memory_space=pltpu.HBM)
    rows = 4 * TILE
    wide = GROUP * SEQ
    return pl.pallas_call(
        main_kernel,
        out_shape=(
            vmem((DEPTH, GROUP * HD), BF16),
            vmem((DEPTH, GROUP * HD), BF16),
            vmem((SEQ, GROUP * HD), BF16),
            vmem((TILE, DEPTH), BF16),
        ),
        in_specs=[held] * 7,
        out_specs=(pl.BlockSpec(memory_space=pltpu.VMEM),) * 4,
        scratch_shapes=[
            vmem((4, TILE, DEPTH), BF16),
            vmem((DEPTH, GROUP * HD), BF16),
            vmem((DEPTH, GROUP * HD), BF16),
            vmem((SEQ, GROUP * HD), BF16),
            vmem((SEQ, GROUP * HD), BF16),
            vmem((8, 8, HALF, HD), F32),
            vmem((8, 8, HALF, HD), F32),
            vmem((8, 4 * HALF + 16, HD), I16),
            vmem((8, 4 * HALF + 16, HD), I16),
            vmem((8, 3, HALF + 16, HD), I16),
            vmem((8, 3, HALF + 16, HD), I16),
            vmem((8, 3, 2, HALF, HD), BF16),
            vmem((8, 3, 2, HALF, HD), BF16),
            vmem((8, HALF, HD), BF16),
            vmem((8, HALF, HD), BF16),
            vmem((8, HALF, HD), F32),
            vmem((rows, HD), BF16),
            vmem((rows, HD), BF16),
            vmem((rows, wide), F32),
            vmem((rows, wide), F32),
            vmem((8, wide), F32),
            vmem((8, wide), F32),
            vmem((8, wide), F32),
            vmem((rows, wide), BF16),
            vmem((TILE, wide), BF16),
            vmem((4, TILE, HD), BF16),
            vmem((4, TILE, HD), BF16),
            vmem((4, TILE, GROUP * HD), BF16),
            vmem((4, TILE, GROUP * HD), BF16),
            vmem((4, 2, HALF, DEPTH), BF16),
            vmem((4, 2, HALF, DEPTH), BF16),
            vmem((TILE, DEPTH), F32),
            vmem((DEPTH, rows), BF16),
            pltpu.SMEM((4,), jnp.int32),
            vmem((1, SEQ), jnp.int32),
            dma((7,)), dma, dma, dma, dma((3, 2)),
            dma((8,)), dma((8,)), dma((6,)), dma((6,)), dma((8,)), dma((8,)),
            dma((4,)), dma((4,)), dma((4,)), dma((2,)), dma,
        ],
        compiler_params=pltpu.CompilerParams(
            collective_id=1, has_side_effects=True, vmem_limit_bytes=VMEM_LIMIT
        ),
        name="main",
    )(count, last, f, wk, wv, q, g)


PIECES = 2


def close_kernel(*refs):
    n = 4
    ins, outs, done = refs[:n], refs[n:2 * n], refs[2 * n]
    copies = []
    for i in range(n):
        rows = ins[i].shape[0] // PIECES
        for j in range(PIECES):
            part = pl.ds(j * rows, rows)
            copies.append(pltpu.make_async_copy(ins[i].at[part], outs[i].at[part], done.at[i, j]))
    for copy in copies:
        copy.start()
    for copy in copies:
        copy.wait()


def close(*arrays):
    n = len(arrays)
    return pl.pallas_call(
        close_kernel,
        out_shape=tuple(jax.ShapeDtypeStruct(x.shape, x.dtype) for x in arrays),
        in_specs=[pl.BlockSpec(memory_space=pltpu.VMEM)] * n,
        out_specs=(pl.BlockSpec(memory_space=pltpu.HBM),) * n,
        scratch_shapes=[pltpu.SemaphoreType.DMA((n, PIECES))],
        compiler_params=pltpu.CompilerParams(vmem_limit_bytes=8 * 2**20),
        name="close",
    )(*arrays)


def per_device(features, key_weight, value_weight, queries, out_grad, tile_count, tile_last):
    kgrad, vgrad, out, fgrad = close(*main(
        tile_count, tile_last.reshape(1, SEQ), features,
        key_weight[0], value_weight[0], queries[0], out_grad[0],
    ))
    return (out[None], fgrad, kgrad[None], vgrad[None])


def solution(mesh):
    in_specs = (
        P(("dp", "section"), "tensor"),
        P("section", "tensor", None),
        P("section", "tensor", None),
        P("section", "dp", "tensor"),
        P("section", "dp", "tensor"),
        P("dp"),
        P("dp"),
    )
    out_specs = (
        P("section", "dp", "tensor"),
        P(("dp", "section"), "tensor"),
        P("section", "tensor", "dp"),
        P("section", "tensor", "dp"),
    )
    return jax.shard_map(
        per_device, mesh=mesh, in_specs=in_specs, out_specs=out_specs, check_vma=False
    )
```

```python
import functools

import jax
import jax.numpy as jnp
from jax import lax
from jax.experimental import pallas as pl
from jax.experimental.pallas import tpu as pltpu
from jax.sharding import PartitionSpec as P

MESH = pl.DeviceIdType.MESH
F32 = jnp.float32
BF16 = jnp.bfloat16
I16 = jnp.int16
HD = 128
GROUP = 8
SECTIONS = 4
RING = 4
TILE = 192
HALF = TILE // 2
DEPTH = 1024
SEQ = 256
LEVELS = 32700.0
FLOOR = -1e30
VMEM_LIMIT = 58 * 2**20


def place():
    t = lax.axis_index("tensor")
    return lax.axis_index("section"), lax.axis_index("dp"), t // 2, lax.rem(t, 2)


def along_x(d):
    s, dp, y, z = place()
    return (lax.rem(s + d, SECTIONS), dp, y * 2 + z)


def along_y(d):
    s, dp, y, z = place()
    return (s, dp, lax.rem(y + d, RING) * 2 + z)


def along_z():
    s, dp, y, z = place()
    return (s, dp, y * 2 + (1 - z))


def greet():
    barrier = pltpu.get_barrier_semaphore()
    peers = [along_x(d) for d in (1, 3)] + [along_y(d) for d in (1, 2, 3)] + [along_z()]
    for peer in peers:
        pl.semaphore_signal(barrier, inc=1, device_id=peer, device_id_type=MESH)
    return barrier, len(peers)


def remote(src, dst, send_sem, recv_sem, device):
    return pltpu.make_async_remote_copy(
        src_ref=src, dst_ref=dst, send_sem=send_sem, recv_sem=recv_sem,
        device_id=device, device_id_type=MESH,
    )


def encode(x):
    top = jnp.maximum(jnp.max(jnp.abs(x), axis=0, keepdims=True), 1e-30)
    power = jnp.ceil(jnp.log(top) * 1.4426950408889634 + 0.0005)
    code = jnp.round(x * (jnp.exp2(-power) * LEVELS)).astype(jnp.int32).astype(I16)
    return code, power


def marks(powers):
    row = lax.broadcasted_iota(jnp.int32, (16, HD), 0)
    mark = jnp.broadcast_to(powers[0], (16, HD))
    for i, power in enumerate(powers[1:]):
        mark = jnp.where(row == i + 1, power, mark)
    return mark.astype(jnp.int32).astype(I16)


def units(mark):
    return jnp.exp2(mark.astype(jnp.int32).astype(F32)) * (1.0 / LEVELS)


def as_f32(code):
    return code.astype(jnp.int32).astype(F32)


ACROSS = (((1,), (1,)), ((), ()))
CHUNKS = ((0, 0), (0, 1), (1, 0), (3, 0), (1, 1), (3, 1), (2, 0), (2, 1))
UNITS = (((2, 0), (2, 1)), ((1, 0), (3, 0)), ((1, 1), (3, 1)), ((0, 0), (0, 1)))
ROWS = sum(UNITS, ())
RELAYED = 6
SLOT = {1: 0, 3: 1, 2: 2}


def ahead_of(i):
    return 1 if i % 2 == 0 else 3


def main_kernel(
    count_hbm, last_hbm, f_ref, wk_ref, wv_ref, q_ref, g_ref,
    kgrad, vgrad, att, fgrad,
    fg, wk, wv, q, g, pk, pv, kz_out, kz_in, ky_out, ky_in, vy_out, vy_in, vz_out, vz_in, sv,
    keys, values, expo, dprobs, tops, sums, dots, probs, dscores, dks, dvs, gk, gv, fs, fr, acc,
    ft, count, last,
    load, out1, out3, x_out, x_in, kz_sem, v1_sem, v2_sem, k1_sem, k2_sem, vz_sem,
    az_sem, by_sem, b2_sem, a2_sem, a3_sem, over_sem, part_sem,
):
    s, dp, y, z = place()
    scale = HD ** -0.5
    loads = [
        pltpu.make_async_copy(src, dst, load.at[i])
        for i, (src, dst) in enumerate((
            (f_ref, fg.at[0]), (wv_ref, wv), (wk_ref, wk), (q_ref, q), (g_ref, g),
            (last_hbm, last), (count_hbm, count),
        ))
    ]
    for copy in loads:
        copy.start()
    barrier, peers = greet()

    def go(*args):
        remote(*args).start()

    def done(ref, sem):
        pltpu.make_async_copy(ref, ref, sem).wait()

    def half(k, h):
        return fg.at[k, pl.ds(h * HALF, HALF)]

    def pass_x(k, h, to, d, sem):
        go(half(k, h), half(to, h), sem, x_in.at[to - 1, h], along_x(d))

    def head_at(d, r):
        return lax.rem(y + d, RING) * 2 + lax.rem(z + r, 2)

    def compute_v(i):
        k, h = CHUNKS[i]
        v = jnp.dot(fg[k, h * HALF:(h + 1) * HALF, :], wv[...], preferred_element_type=F32)
        for head in range(8):
            pv[i, head] = v[:, head * HD:(head + 1) * HD]
        for d in (2, RING - ahead_of(i)) if i < RELAYED else (2, 1, 3):
            for r in range(2):
                vy_out[i, SLOT[d], r] = pv[i, head_at(d, r)].astype(BF16)

    def compute_k(i):
        k, h = CHUNKS[i]
        p = jnp.dot(fg[k, h * HALF:(h + 1) * HALF, :], wk[...], preferred_element_type=F32)
        for head in range(8):
            pk[i, head] = p[:, head * HD:(head + 1) * HD]
        powers = []
        for d in range(RING):
            code, power = encode(pk[i, head_at(d, 1)])
            kz_out[i, d * HALF:(d + 1) * HALF, :] = code
            powers.append(power)
        kz_out[i, 4 * HALF:4 * HALF + 16, :] = marks(powers)

    def send_y(i, d, to, at, sem):
        go(vy_out.at[i, SLOT[d]], vy_in.at[i, SLOT[at]], out1, sem.at[i], along_y(to))

    def send_v(i):
        ahead = ahead_of(i)
        if i < RELAYED:
            send_y(i, 2, ahead, 2, v1_sem)
            send_y(i, RING - ahead, RING - ahead, ahead, v2_sem)
        else:
            for d in (2, 1, 3):
                send_y(i, d, d, RING - d, v1_sem)

    def send_z(i):
        go(kz_out.at[i], kz_in.at[i], out1, kz_sem.at[i], along_z())

    def start(i):
        k, h = CHUNKS[i]
        if k == 2:
            done(half(k, h), x_in.at[k - 1, h])
        compute_v(i)
        send_v(i)
        compute_k(i)
        send_z(i)

    def send_k(i, d, to, at, total, sem):
        code, power = encode(total)
        ky_out[i, SLOT[d], 0:HALF, :] = code
        ky_out[i, SLOT[d], HALF:HALF + 16, :] = marks([power])
        go(ky_out.at[i, SLOT[d]], ky_in.at[i, SLOT[at]], out1, sem.at[i], along_y(to))

    def got_k(i, at):
        unit = units(ky_in[i, at, HALF:HALF + 16, :])
        return as_f32(ky_in[i, at, 0:HALF, :]) * unit[0:1]

    def gather_v(i, n, sem):
        done(vy_in.at[i, pl.ds(0, n)], sem.at[i])
        for r in (1, 0):
            total = pv[i, head_at(0, r)]
            for at in range(n):
                total = total + vy_in[i, at, r].astype(F32)
            if r:
                vz_out[i] = total.astype(BF16)
                go(vz_out.at[i], vz_in.at[i], out1, vz_sem.at[i], along_z())
            else:
                sv[i] = total

    def middle(i):
        ahead = ahead_of(i)
        behind = RING - ahead
        if i < RELAYED:
            done(vy_in.at[i, 2], v1_sem.at[i])
            for r in range(2):
                total = pv[i, head_at(ahead, r)] + vy_in[i, 2, r].astype(F32)
                vy_out[i, SLOT[ahead], r] = total.astype(BF16)
            send_y(i, ahead, ahead, behind, v2_sem)
        done(kz_in.at[i], kz_sem.at[i])
        unit = units(kz_in[i, 4 * HALF:4 * HALF + 16, :])
        for d in (2, 1, 3, 0):
            head = head_at(d, 0)
            total = pk[i, head] + as_f32(kz_in[i, d * HALF:(d + 1) * HALF, :]) * unit[d:d + 1]
            if i >= RELAYED and d:
                send_k(i, d, d, RING - d, total, k2_sem)
            elif d == 2:
                send_k(i, 2, behind, 2, total, k1_sem)
            elif d == ahead:
                send_k(i, ahead, ahead, behind, total, k2_sem)
            else:
                pk[i, head] = total
        if i >= RELAYED:
            gather_v(i, 3, v1_sem)

    def relay(i):
        ahead = ahead_of(i)
        behind = RING - ahead
        done(ky_in.at[i, 2], k1_sem.at[i])
        send_k(i, behind, behind, ahead, pk[i, head_at(behind, 0)] + got_k(i, 2), k2_sem)
        gather_v(i, 2, v2_sem)

    def finish(i):
        k, h = CHUNKS[i]
        at = ROWS.index((k, h)) * HALF
        spot = slice(at, at + HALF)
        n = 2 if i < RELAYED else 3
        done(ky_in.at[i, pl.ds(0, n)], k2_sem.at[i])
        total = pk[i, head_at(0, 0)]
        for at in range(n):
            total = total + got_k(i, at)
        key = total.astype(BF16)
        keys[spot, :] = key
        done(vz_in.at[i], vz_sem.at[i])
        value = (sv[i] + vz_in[i].astype(F32)).astype(BF16)
        values[spot, :] = value
        tile = lax.rem(s + k, SECTIONS)
        slot = lax.broadcasted_iota(jnp.int32, (HALF, SEQ), 0) + h * HALF
        limit = jnp.where(slot < count[tile], tile, SECTIONS)
        visible = limit <= last[...]
        for j in range(GROUP):
            cols = slice(j * HD, (j + 1) * HD)
            wide = slice(j * SEQ, (j + 1) * SEQ)
            scores = lax.dot_general(key, q[:, cols], ACROSS, preferred_element_type=F32) * scale
            masked = jnp.where(visible, scores, -jnp.inf)
            top = jnp.maximum(jnp.max(masked, axis=0, keepdims=True), FLOOR)
            e = jnp.exp(masked - top)
            dprob = lax.dot_general(value, g[:, cols], ACROSS, preferred_element_type=F32)
            expo[spot, wide] = e
            dprobs[spot, wide] = dprob
            tops[i:i + 1, wide] = top
            sums[i:i + 1, wide] = jnp.sum(e, axis=0, keepdims=True)
            dots[i:i + 1, wide] = jnp.sum(e * dprob, axis=0, keepdims=True)

    def turn(a):
        rows = [fg[k, h * HALF:(h + 1) * HALF, :] for k, h in ROWS[4 * a:4 * a + 4]]
        ft[:, a * 2 * TILE:(a + 1) * 2 * TILE] = jnp.concatenate(rows, axis=0).T

    loads[0].wait()
    loads[1].wait()
    compute_v(0)
    pl.semaphore_wait(barrier, peers)
    pass_x(0, 0, 3, 1, x_out)
    pass_x(0, 0, 1, 3, x_out)
    send_v(0)
    loads[2].wait()
    compute_k(0)
    send_z(0)
    start(1)
    middle(0)
    done(fg.at[0], x_out)
    pass_x(0, 1, 3, 1, out1)
    pass_x(0, 1, 1, 3, out1)
    middle(1)
    done(half(1, 0), x_in.at[0, 0])
    start(2)
    done(half(3, 0), x_in.at[2, 0])
    start(3)
    relay(0)
    relay(1)
    for copy in loads[3:]:
        copy.wait()
    done(half(1, 1), x_in.at[0, 1])
    pass_x(1, 0, 2, 3, out1)
    done(half(3, 1), x_in.at[2, 1])
    pass_x(3, 1, 2, 1, out1)
    start(4)
    middle(2)
    start(5)
    middle(3)
    relay(2)
    finish(0)
    finish(1)
    start(6)
    middle(4)
    relay(3)
    start(7)
    middle(5)
    relay(4)
    finish(2)
    middle(6)
    relay(5)
    finish(3)
    middle(7)
    finish(4)
    turn(0)
    turn(1)
    finish(5)
    finish(6)
    finish(7)

    peak = jnp.max(tops[...], axis=0, keepdims=True)
    share = jnp.exp(tops[...] - peak)
    inverse = 1.0 / jnp.sum(share * sums[...], axis=0, keepdims=True)
    share = share * inverse
    sums[...] = share
    dots[0:1, :] = jnp.sum(share * dots[...], axis=0, keepdims=True)

    mine = y * 2 + z

    def heads(ref, k):
        return jnp.concatenate([ref[k, head] for head in range(8)], axis=1)

    def attend(k):
        dk = dv = None
        for j in range(GROUP):
            narrow = slice(j * HD, (j + 1) * HD)
            wide = slice(j * SEQ, (j + 1) * SEQ)
            delta = dots[0:1, wide]
            for h in range(2):
                i = CHUNKS.index(UNITS[k][h])
                spot = slice(k * TILE + h * HALF, k * TILE + (h + 1) * HALF)
                p = expo[spot, wide] * sums[i:i + 1, wide]
                probs[spot, wide] = p.astype(BF16)
                dscores[h * HALF:(h + 1) * HALF, wide] = (p * (dprobs[spot, wide] - delta) * scale).astype(BF16)
            whole = slice(k * TILE, (k + 1) * TILE)
            dv_j = jnp.dot(probs[whole, wide], g[:, narrow], preferred_element_type=F32)
            dk_j = jnp.dot(dscores[:, wide], q[:, narrow], preferred_element_type=F32)
            dv = dv_j if j == 0 else dv + dv_j
            dk = dk_j if j == 0 else dk + dk_j
        for ref, into, value in ((dvs, gv, dv), (dks, gk, dk)):
            rounded = value.astype(BF16)
            ref[k] = rounded
            into[k, mine] = rounded

    def ways(k):
        return (1, 3) if k % 2 == 0 else (3, 1)

    def zero(k):
        for d in (1, 3):
            go(dvs.at[k], gv.at[k, mine], out3, by_sem.at[k, SLOT[RING - d]], along_y(d))
        go(dks.at[k], gk.at[k, mine], out3, az_sem.at[k], along_z())
        go(dvs.at[k], gv.at[k, mine], out3, a3_sem.at[k], along_z())

    def one(k):
        ahead, behind = ways(k)
        done(gk.at[k, 0], az_sem.at[k])
        pair = pl.ds(y * 2, 2)
        go(gk.at[k, pair], gk.at[k, pair], out3, a2_sem.at[k], along_y(ahead))
        go(gk.at[k, pair], gk.at[k, pair], out3, a3_sem.at[k], along_y(behind))
        for d in (behind, ahead):
            done(gv.at[k, 0], by_sem.at[k, SLOT[d]])
            head = head_at(d, 0)
            if d == behind:
                go(gv.at[k, head], gv.at[k, head], out3, b2_sem.at[k], along_y(ahead))
            go(gv.at[k, head], gv.at[k, head], out3, a3_sem.at[k], along_z())

    def two(k):
        ahead, behind = ways(k)
        done(gk.at[k, pl.ds(0, 2)], a2_sem.at[k])
        pair = pl.ds(lax.rem(y + behind, RING) * 2, 2)
        go(gk.at[k, pair], gk.at[k, pair], out3, a3_sem.at[k], along_y(ahead))
        done(gv.at[k, 0], b2_sem.at[k])
        head = head_at(2, 0)
        go(gv.at[k, head], gv.at[k, head], out3, a3_sem.at[k], along_z())

    def three(k):
        done(gk.at[k], a3_sem.at[k])
        total = lax.dot_general(heads(gk, k), wk[...], ACROSS, preferred_element_type=F32)
        total += lax.dot_general(heads(gv, k), wv[...], ACROSS, preferred_element_type=F32)
        for h, (tile, part) in enumerate(UNITS[k]):
            half_total = total[h * HALF:(h + 1) * HALF]
            if tile == 0:
                acc[h * HALF:(h + 1) * HALF, :] = half_total
                continue
            way = tile if tile != 2 else (3, 1)[part]
            if (tile, part) in ((1, 1), (3, 0)):
                done(fr.at[2, part], over_sem.at[part])
                half_total = half_total + fr[2, part].astype(F32)
            fs[tile, part] = half_total.astype(BF16)
            if tile == 2:
                go(fs.at[tile, part], fr.at[2, part], out3, over_sem.at[part], along_x(way))
            else:
                go(fs.at[tile, part], fr.at[SLOT[SECTIONS - way], part], out3, part_sem, along_x(way))

    def weights(a, j):
        rows = slice(a * 2 * TILE, (a + 1) * 2 * TILE)
        side = slice(j * DEPTH, (j + 1) * DEPTH)
        src, dst = ((gk, kgrad), (gv, vgrad))[j]
        rhs = jnp.concatenate([heads(src, 2 * a), heads(src, 2 * a + 1)], axis=0)
        total = jnp.dot(ft[:, rows], rhs, preferred_element_type=F32)
        if a == 0:
            expo[0:3 * SEQ, side] = total[0:3 * SEQ]
            dprobs[0:SEQ, side] = total[3 * SEQ:4 * SEQ]
        else:
            dst[0:3 * SEQ, :] = (expo[0:3 * SEQ, side] + total[0:3 * SEQ]).astype(BF16)
            dst[3 * SEQ:4 * SEQ, :] = (dprobs[0:SEQ, side] + total[3 * SEQ:4 * SEQ]).astype(BF16)

    def forward():
        turned = values[...].T
        for j in range(GROUP):
            out = jnp.dot(turned, probs[:, j * SEQ:(j + 1) * SEQ], preferred_element_type=F32)
            att[:, j * HD:(j + 1) * HD] = out.T.astype(BF16)

    attend(0)
    zero(0)
    attend(1)
    zero(1)
    one(0)
    attend(2)
    zero(2)
    one(1)
    two(0)
    attend(3)
    zero(3)
    one(2)
    two(1)
    three(0)
    one(3)
    two(2)
    forward()
    three(1)
    two(3)
    weights(0, 0)
    three(2)
    weights(0, 1)
    three(3)
    weights(1, 0)
    weights(1, 1)
    done(fr.at[pl.ds(0, 2)], part_sem)
    for h in range(2):
        rows = slice(h * HALF, (h + 1) * HALF)
        total = acc[rows, :]
        for at in (0, 1):
            total = total + fr[at, h].astype(F32)
        fgrad[rows, :] = total.astype(BF16)
    done(expo.at[pl.ds(0, 448)], out1)
    done(expo.at[pl.ds(0, 480)], out3)


def main(count, last, f, wk, wv, q, g):
    dma = pltpu.SemaphoreType.DMA
    vmem = pltpu.VMEM
    held = pl.BlockSpec(memory_space=pltpu.HBM)
    rows = 4 * TILE
    wide = GROUP * SEQ
    return pl.pallas_call(
        main_kernel,
        out_shape=(
            vmem((DEPTH, GROUP * HD), BF16),
            vmem((DEPTH, GROUP * HD), BF16),
            vmem((SEQ, GROUP * HD), BF16),
            vmem((TILE, DEPTH), BF16),
        ),
        in_specs=[held] * 7,
        out_specs=(pl.BlockSpec(memory_space=pltpu.VMEM),) * 4,
        scratch_shapes=[
            vmem((4, TILE, DEPTH), BF16),
            vmem((DEPTH, GROUP * HD), BF16),
            vmem((DEPTH, GROUP * HD), BF16),
            vmem((SEQ, GROUP * HD), BF16),
            vmem((SEQ, GROUP * HD), BF16),
            vmem((8, 8, HALF, HD), F32),
            vmem((8, 8, HALF, HD), F32),
            vmem((8, 4 * HALF + 16, HD), I16),
            vmem((8, 4 * HALF + 16, HD), I16),
            vmem((8, 3, HALF + 16, HD), I16),
            vmem((8, 3, HALF + 16, HD), I16),
            vmem((8, 3, 2, HALF, HD), BF16),
            vmem((8, 3, 2, HALF, HD), BF16),
            vmem((8, HALF, HD), BF16),
            vmem((8, HALF, HD), BF16),
            vmem((8, HALF, HD), F32),
            vmem((rows, HD), BF16),
            vmem((rows, HD), BF16),
            vmem((rows, wide), F32),
            vmem((rows, wide), F32),
            vmem((8, wide), F32),
            vmem((8, wide), F32),
            vmem((8, wide), F32),
            vmem((rows, wide), BF16),
            vmem((TILE, wide), BF16),
            vmem((4, TILE, HD), BF16),
            vmem((4, TILE, HD), BF16),
            vmem((4, 8, TILE, HD), BF16),
            vmem((4, 8, TILE, HD), BF16),
            vmem((4, 2, HALF, DEPTH), BF16),
            vmem((4, 2, HALF, DEPTH), BF16),
            vmem((TILE, DEPTH), F32),
            vmem((DEPTH, rows), BF16),
            pltpu.SMEM((4,), jnp.int32),
            vmem((1, SEQ), jnp.int32),
            dma((7,)), dma, dma, dma, dma((3, 2)),
            dma((8,)), dma((8,)), dma((6,)), dma((6,)), dma((8,)), dma((8,)),
            dma((4,)), dma((4, 2)), dma((4,)), dma((4,)), dma((4,)), dma((2,)), dma,
        ],
        compiler_params=pltpu.CompilerParams(
            collective_id=1, has_side_effects=True, vmem_limit_bytes=VMEM_LIMIT
        ),
        name="main",
    )(count, last, f, wk, wv, q, g)


PIECES = 2


def close_kernel(*refs):
    n = 4
    ins, outs, done = refs[:n], refs[n:2 * n], refs[2 * n]
    copies = []
    for i in range(n):
        rows = ins[i].shape[0] // PIECES
        for j in range(PIECES):
            part = pl.ds(j * rows, rows)
            copies.append(pltpu.make_async_copy(ins[i].at[part], outs[i].at[part], done.at[i, j]))
    for copy in copies:
        copy.start()
    for copy in copies:
        copy.wait()


def close(*arrays):
    n = len(arrays)
    return pl.pallas_call(
        close_kernel,
        out_shape=tuple(jax.ShapeDtypeStruct(x.shape, x.dtype) for x in arrays),
        in_specs=[pl.BlockSpec(memory_space=pltpu.VMEM)] * n,
        out_specs=(pl.BlockSpec(memory_space=pltpu.HBM),) * n,
        scratch_shapes=[pltpu.SemaphoreType.DMA((n, PIECES))],
        compiler_params=pltpu.CompilerParams(vmem_limit_bytes=8 * 2**20),
        name="close",
    )(*arrays)


def per_device(features, key_weight, value_weight, queries, out_grad, tile_count, tile_last):
    kgrad, vgrad, out, fgrad = close(*main(
        tile_count, tile_last.reshape(1, SEQ), features,
        key_weight[0], value_weight[0], queries[0], out_grad[0],
    ))
    return (out[None], fgrad, kgrad[None], vgrad[None])


def solution(mesh):
    in_specs = (
        P(("dp", "section"), "tensor"),
        P("section", "tensor", None),
        P("section", "tensor", None),
        P("section", "dp", "tensor"),
        P("section", "dp", "tensor"),
        P("dp"),
        P("dp"),
    )
    out_specs = (
        P("section", "dp", "tensor"),
        P(("dp", "section"), "tensor"),
        P("section", "tensor", "dp"),
        P("section", "tensor", "dp"),
    )
    return jax.shard_map(
        per_device, mesh=mesh, in_specs=in_specs, out_specs=out_specs, check_vma=False
    )
```

```python
import functools

import jax
import jax.numpy as jnp
from jax import lax
from jax.experimental import pallas as pl
from jax.experimental.pallas import tpu as pltpu
from jax.sharding import PartitionSpec as P

MESH = pl.DeviceIdType.MESH
F32 = jnp.float32
BF16 = jnp.bfloat16
I16 = jnp.int16
HD = 128
GROUP = 8
SECTIONS = 4
RING = 4
TILE = 192
HALF = TILE // 2
PITCH = 256
DEPTH = 1024
SEQ = 256
LEVELS = 32700.0
FLOOR = -1e30
VMEM_LIMIT = 58 * 2**20


def place():
    t = lax.axis_index("tensor")
    return lax.axis_index("section"), lax.axis_index("dp"), t // 2, lax.rem(t, 2)


def along_x(d):
    s, dp, y, z = place()
    return (lax.rem(s + d, SECTIONS), dp, y * 2 + z)


def along_y(d):
    s, dp, y, z = place()
    return (s, dp, lax.rem(y + d, RING) * 2 + z)


def along_z():
    s, dp, y, z = place()
    return (s, dp, y * 2 + (1 - z))


def greet():
    barrier = pltpu.get_barrier_semaphore()
    peers = [along_x(d) for d in (1, 3)] + [along_y(d) for d in (1, 2, 3)] + [along_z()]
    for peer in peers:
        pl.semaphore_signal(barrier, inc=1, device_id=peer, device_id_type=MESH)
    return barrier, len(peers)


def remote(src, dst, send_sem, recv_sem, device):
    return pltpu.make_async_remote_copy(
        src_ref=src, dst_ref=dst, send_sem=send_sem, recv_sem=recv_sem,
        device_id=device, device_id_type=MESH,
    )


def encode(x):
    top = jnp.maximum(jnp.max(jnp.abs(x), axis=0, keepdims=True), 1e-30)
    power = jnp.ceil(jnp.log(top) * 1.4426950408889634 + 0.0005)
    code = jnp.round(x * (jnp.exp2(-power) * LEVELS)).astype(jnp.int32).astype(I16)
    return code, power


def marks(powers):
    row = lax.broadcasted_iota(jnp.int32, (16, HD), 0)
    mark = jnp.broadcast_to(powers[0], (16, HD))
    for i, power in enumerate(powers[1:]):
        mark = jnp.where(row == i + 1, power, mark)
    return mark.astype(jnp.int32).astype(I16)


def units(mark):
    return jnp.exp2(mark.astype(jnp.int32).astype(F32)) * (1.0 / LEVELS)


def as_f32(code):
    return code.astype(jnp.int32).astype(F32)


ACROSS = (((1,), (1,)), ((), ()))
CHUNKS = ((0, 0), (0, 1), (1, 0), (3, 0), (1, 1), (3, 1), (2, 0), (2, 1))
UNITS = (((2, 0), (2, 1)), ((1, 0), (3, 0)), ((1, 1), (3, 1)), ((0, 0), (0, 1)))
ROWS = sum(UNITS, ())
RELAYED = 6
SLOT = {1: 0, 3: 1, 2: 2}


def ahead_of(i):
    return 1 if i % 2 == 0 else 3


def main_kernel(
    count_hbm, last_hbm, f_ref, wk_ref, wv_ref, q_ref, g_ref,
    kgrad, vgrad, att, fgrad,
    fg, wk, wv, q, g, pk, pv, kz_out, kz_in, ky_out, ky_in, vy_out, vy_in, vz_out, vz_in, sv,
    keys, values, expo, dprobs, tops, sums, dots, probs, dscores, dks, dvs, gk, gv, fs, fr, acc,
    ft, count, last,
    load, out1, out3, x_out, x_in, kz_sem, v1_sem, v2_sem, k1_sem, k2_sem, vz_sem,
    az_sem, by_sem, b2_sem, a2_sem, a3_sem, over_sem, part_sem,
):
    s, dp, y, z = place()
    scale = HD ** -0.5
    loads = [
        pltpu.make_async_copy(src, dst, load.at[i])
        for i, (src, dst) in enumerate((
            (f_ref, fg.at[0]), (wv_ref, wv), (wk_ref, wk), (q_ref, q), (g_ref, g),
            (last_hbm, last), (count_hbm, count),
        ))
    ]
    for copy in loads:
        copy.start()
    barrier, peers = greet()

    def go(*args):
        remote(*args).start()

    def done(ref, sem):
        pltpu.make_async_copy(ref, ref, sem).wait()

    def half(k, h):
        return fg.at[k, pl.ds(h * HALF, HALF)]

    def pass_x(k, h, to, d, sem):
        go(half(k, h), half(to, h), sem, x_in.at[to - 1, h], along_x(d))

    def head_at(d, r):
        return lax.rem(y + d, RING) * 2 + lax.rem(z + r, 2)

    def compute_v(i):
        k, h = CHUNKS[i]
        v = jnp.dot(fg[k, h * HALF:(h + 1) * HALF, :], wv[...], preferred_element_type=F32)
        for head in range(8):
            pv[i, head] = v[:, head * HD:(head + 1) * HD]
        for d in (2, RING - ahead_of(i)) if i < RELAYED else (2, 1, 3):
            for r in range(2):
                vy_out[i, SLOT[d], r] = pv[i, head_at(d, r)].astype(BF16)

    def compute_k(i):
        k, h = CHUNKS[i]
        p = jnp.dot(fg[k, h * HALF:(h + 1) * HALF, :], wk[...], preferred_element_type=F32)
        for head in range(8):
            pk[i, head] = p[:, head * HD:(head + 1) * HD]
        powers = []
        for d in range(RING):
            code, power = encode(pk[i, head_at(d, 1)])
            kz_out[i, d * HALF:(d + 1) * HALF, :] = code
            powers.append(power)
        kz_out[i, 4 * HALF:4 * HALF + 16, :] = marks(powers)

    def send_y(i, d, to, at, sem):
        go(vy_out.at[i, SLOT[d]], vy_in.at[i, SLOT[at]], out1, sem.at[i], along_y(to))

    def send_v(i):
        ahead = ahead_of(i)
        if i < RELAYED:
            send_y(i, 2, ahead, 2, v1_sem)
            send_y(i, RING - ahead, RING - ahead, ahead, v2_sem)
        else:
            for d in (2, 1, 3):
                send_y(i, d, d, RING - d, v1_sem)

    def send_z(i):
        go(kz_out.at[i], kz_in.at[i], out1, kz_sem.at[i], along_z())

    def start(i):
        k, h = CHUNKS[i]
        if k == 2:
            done(half(k, h), x_in.at[k - 1, h])
        compute_v(i)
        send_v(i)
        compute_k(i)
        send_z(i)

    def send_k(i, d, to, at, total, sem):
        code, power = encode(total)
        ky_out[i, SLOT[d], 0:HALF, :] = code
        ky_out[i, SLOT[d], HALF:HALF + 16, :] = marks([power])
        go(ky_out.at[i, SLOT[d]], ky_in.at[i, SLOT[at]], out1, sem.at[i], along_y(to))

    def got_k(i, at):
        unit = units(ky_in[i, at, HALF:HALF + 16, :])
        return as_f32(ky_in[i, at, 0:HALF, :]) * unit[0:1]

    def gather_v(i, n, sem):
        done(vy_in.at[i, pl.ds(0, n)], sem.at[i])
        for r in (1, 0):
            total = pv[i, head_at(0, r)]
            for at in range(n):
                total = total + vy_in[i, at, r].astype(F32)
            if r:
                vz_out[i] = total.astype(BF16)
                go(vz_out.at[i], vz_in.at[i], out1, vz_sem.at[i], along_z())
            else:
                sv[i] = total

    def middle(i):
        ahead = ahead_of(i)
        behind = RING - ahead
        if i < RELAYED:
            done(vy_in.at[i, 2], v1_sem.at[i])
            for r in range(2):
                total = pv[i, head_at(ahead, r)] + vy_in[i, 2, r].astype(F32)
                vy_out[i, SLOT[ahead], r] = total.astype(BF16)
            send_y(i, ahead, ahead, behind, v2_sem)
        done(kz_in.at[i], kz_sem.at[i])
        unit = units(kz_in[i, 4 * HALF:4 * HALF + 16, :])
        for d in (2, 1, 3, 0):
            head = head_at(d, 0)
            total = pk[i, head] + as_f32(kz_in[i, d * HALF:(d + 1) * HALF, :]) * unit[d:d + 1]
            if i >= RELAYED and d:
                send_k(i, d, d, RING - d, total, k2_sem)
            elif d == 2:
                send_k(i, 2, behind, 2, total, k1_sem)
            elif d == ahead:
                send_k(i, ahead, ahead, behind, total, k2_sem)
            else:
                pk[i, head] = total
        if i >= RELAYED:
            gather_v(i, 3, v1_sem)

    def relay(i):
        ahead = ahead_of(i)
        behind = RING - ahead
        done(ky_in.at[i, 2], k1_sem.at[i])
        send_k(i, behind, behind, ahead, pk[i, head_at(behind, 0)] + got_k(i, 2), k2_sem)
        gather_v(i, 2, v2_sem)

    def finish(i):
        k, h = CHUNKS[i]
        at = ROWS.index((k, h)) * HALF
        spot = slice(at, at + HALF)
        n = 2 if i < RELAYED else 3
        done(ky_in.at[i, pl.ds(0, n)], k2_sem.at[i])
        total = pk[i, head_at(0, 0)]
        for at in range(n):
            total = total + got_k(i, at)
        key = total.astype(BF16)
        keys[spot, :] = key
        done(vz_in.at[i], vz_sem.at[i])
        value = (sv[i] + vz_in[i].astype(F32)).astype(BF16)
        values[spot, :] = value
        tile = lax.rem(s + k, SECTIONS)
        slot = lax.broadcasted_iota(jnp.int32, (HALF, SEQ), 0) + h * HALF
        limit = jnp.where(slot < count[tile], tile, SECTIONS)
        visible = limit <= last[...]
        for j in range(GROUP):
            cols = slice(j * HD, (j + 1) * HD)
            wide = slice(j * SEQ, (j + 1) * SEQ)
            scores = lax.dot_general(key, q[:, cols], ACROSS, preferred_element_type=F32) * scale
            masked = jnp.where(visible, scores, -jnp.inf)
            top = jnp.maximum(jnp.max(masked, axis=0, keepdims=True), FLOOR)
            e = jnp.exp(masked - top)
            dprob = lax.dot_general(value, g[:, cols], ACROSS, preferred_element_type=F32)
            expo[spot, wide] = e
            dprobs[spot, wide] = dprob
            tops[i:i + 1, wide] = top
            sums[i:i + 1, wide] = jnp.sum(e, axis=0, keepdims=True)
            dots[i:i + 1, wide] = jnp.sum(e * dprob, axis=0, keepdims=True)

    def turn(k):
        rows = [fg[tile, h * HALF:(h + 1) * HALF, :] for tile, h in UNITS[k]]
        ft[:, k * PITCH:k * PITCH + TILE] = jnp.concatenate(rows, axis=0).T

    loads[0].wait()
    loads[1].wait()
    compute_v(0)
    pl.semaphore_wait(barrier, peers)
    pass_x(0, 0, 3, 1, x_out)
    pass_x(0, 0, 1, 3, x_out)
    send_v(0)
    loads[2].wait()
    compute_k(0)
    send_z(0)
    start(1)
    middle(0)
    done(fg.at[0], x_out)
    pass_x(0, 1, 3, 1, out1)
    pass_x(0, 1, 1, 3, out1)
    middle(1)
    done(half(1, 0), x_in.at[0, 0])
    start(2)
    done(half(3, 0), x_in.at[2, 0])
    start(3)
    relay(0)
    relay(1)
    for copy in loads[3:]:
        copy.wait()
    done(half(1, 1), x_in.at[0, 1])
    pass_x(1, 0, 2, 3, out1)
    done(half(3, 1), x_in.at[2, 1])
    pass_x(3, 1, 2, 1, out1)
    start(4)
    middle(2)
    start(5)
    middle(3)
    relay(2)
    finish(0)
    finish(1)
    start(6)
    middle(4)
    relay(3)
    start(7)
    middle(5)
    relay(4)
    middle(6)
    middle(7)
    relay(5)
    finish(2)
    finish(3)
    finish(4)
    finish(5)
    finish(6)
    finish(7)

    peak = jnp.max(tops[...], axis=0, keepdims=True)
    share = jnp.exp(tops[...] - peak)
    inverse = 1.0 / jnp.sum(share * sums[...], axis=0, keepdims=True)
    share = share * inverse
    sums[...] = share
    dots[0:1, :] = jnp.sum(share * dots[...], axis=0, keepdims=True)

    mine = y * 2 + z

    def heads(ref, k):
        return jnp.concatenate([ref[k, head] for head in range(8)], axis=1)

    def attend(k):
        dk = dv = None
        for j in range(GROUP):
            narrow = slice(j * HD, (j + 1) * HD)
            wide = slice(j * SEQ, (j + 1) * SEQ)
            delta = dots[0:1, wide]
            for h in range(2):
                i = CHUNKS.index(UNITS[k][h])
                spot = slice(k * TILE + h * HALF, k * TILE + (h + 1) * HALF)
                p = expo[spot, wide] * sums[i:i + 1, wide]
                probs[spot, wide] = p.astype(BF16)
                dscores[h * HALF:(h + 1) * HALF, wide] = (p * (dprobs[spot, wide] - delta) * scale).astype(BF16)
            whole = slice(k * TILE, (k + 1) * TILE)
            dv_j = jnp.dot(probs[whole, wide], g[:, narrow], preferred_element_type=F32)
            dk_j = jnp.dot(dscores[:, wide], q[:, narrow], preferred_element_type=F32)
            dv = dv_j if j == 0 else dv + dv_j
            dk = dk_j if j == 0 else dk + dk_j
        for ref, into, value in ((dvs, gv, dv), (dks, gk, dk)):
            rounded = value.astype(BF16)
            ref[k] = rounded
            into[k, mine] = rounded

    def ways(k):
        return (1, 3) if k % 2 == 0 else (3, 1)

    def zero(k):
        for d in (1, 3):
            go(dvs.at[k], gv.at[k, mine], out3, by_sem.at[k, SLOT[RING - d]], along_y(d))
        go(dks.at[k], gk.at[k, mine], out3, az_sem.at[k], along_z())
        go(dvs.at[k], gv.at[k, mine], out3, a3_sem.at[k], along_z())

    def one(k):
        ahead, behind = ways(k)
        done(gk.at[k, 0], az_sem.at[k])
        pair = pl.ds(y * 2, 2)
        go(gk.at[k, pair], gk.at[k, pair], out3, a2_sem.at[k], along_y(ahead))
        go(gk.at[k, pair], gk.at[k, pair], out3, a3_sem.at[k], along_y(behind))
        for d in (behind, ahead):
            done(gv.at[k, 0], by_sem.at[k, SLOT[d]])
            head = head_at(d, 0)
            if d == behind:
                go(gv.at[k, head], gv.at[k, head], out3, b2_sem.at[k], along_y(ahead))
            go(gv.at[k, head], gv.at[k, head], out3, a3_sem.at[k], along_z())

    def two(k):
        ahead, behind = ways(k)
        done(gk.at[k, pl.ds(0, 2)], a2_sem.at[k])
        pair = pl.ds(lax.rem(y + behind, RING) * 2, 2)
        go(gk.at[k, pair], gk.at[k, pair], out3, a3_sem.at[k], along_y(ahead))
        done(gv.at[k, 0], b2_sem.at[k])
        head = head_at(2, 0)
        go(gv.at[k, head], gv.at[k, head], out3, a3_sem.at[k], along_z())

    def three(k):
        done(gk.at[k], a3_sem.at[k])
        total = lax.dot_general(heads(gk, k), wk[...], ACROSS, preferred_element_type=F32)
        total += lax.dot_general(heads(gv, k), wv[...], ACROSS, preferred_element_type=F32)
        for h, (tile, part) in enumerate(UNITS[k]):
            half_total = total[h * HALF:(h + 1) * HALF]
            if tile == 0:
                acc[h * HALF:(h + 1) * HALF, :] = half_total
                continue
            way = tile if tile != 2 else (3, 1)[part]
            if (tile, part) in ((1, 1), (3, 0)):
                done(fr.at[2, part], over_sem.at[part])
                half_total = half_total + fr[2, part].astype(F32)
            fs[tile, part] = half_total.astype(BF16)
            if tile == 2:
                go(fs.at[tile, part], fr.at[2, part], out3, over_sem.at[part], along_x(way))
            else:
                go(fs.at[tile, part], fr.at[SLOT[SECTIONS - way], part], out3, part_sem, along_x(way))

    def weights(k):
        for j, (src, dst) in enumerate(((gk, kgrad), (gv, vgrad))):
            side = slice(j * DEPTH, (j + 1) * DEPTH)
            total = jnp.dot(ft[:, k * PITCH:k * PITCH + TILE], heads(src, k), preferred_element_type=F32)
            for held, out in (
                (expo.at[0:3 * SEQ, side], slice(0, 3 * SEQ)),
                (dprobs.at[0:SEQ, side], slice(3 * SEQ, 4 * SEQ)),
            ):
                if k == 0:
                    held[...] = total[out]
                elif k < 3:
                    held[...] += total[out]
                else:
                    dst[out, :] = (held[...] + total[out]).astype(BF16)

    def forward():
        turned = values[...].T
        for j in range(GROUP):
            out = jnp.dot(turned, probs[:, j * SEQ:(j + 1) * SEQ], preferred_element_type=F32)
            att[:, j * HD:(j + 1) * HD] = out.T.astype(BF16)

    attend(0)
    zero(0)
    attend(1)
    zero(1)
    for k in range(4):
        turn(k)
    attend(2)
    one(0)
    zero(2)
    attend(3)
    one(1)
    two(0)
    zero(3)
    one(2)
    two(1)
    one(3)
    two(2)
    three(0)
    forward()
    weights(0)
    two(3)
    three(1)
    three(2)
    three(3)
    weights(1)
    weights(2)
    weights(3)
    done(fr.at[pl.ds(0, 2)], part_sem)
    for h in range(2):
        rows = slice(h * HALF, (h + 1) * HALF)
        total = acc[rows, :]
        for at in (0, 1):
            total = total + fr[at, h].astype(F32)
        fgrad[rows, :] = total.astype(BF16)
    done(expo.at[pl.ds(0, 448)], out1)
    done(expo.at[pl.ds(0, 480)], out3)


def main(count, last, f, wk, wv, q, g):
    dma = pltpu.SemaphoreType.DMA
    vmem = pltpu.VMEM
    held = pl.BlockSpec(memory_space=pltpu.HBM)
    rows = 4 * TILE
    wide = GROUP * SEQ
    return pl.pallas_call(
        main_kernel,
        out_shape=(
            vmem((DEPTH, GROUP * HD), BF16),
            vmem((DEPTH, GROUP * HD), BF16),
            vmem((SEQ, GROUP * HD), BF16),
            vmem((TILE, DEPTH), BF16),
        ),
        in_specs=[held] * 7,
        out_specs=(pl.BlockSpec(memory_space=pltpu.VMEM),) * 4,
        scratch_shapes=[
            vmem((4, TILE, DEPTH), BF16),
            vmem((DEPTH, GROUP * HD), BF16),
            vmem((DEPTH, GROUP * HD), BF16),
            vmem((SEQ, GROUP * HD), BF16),
            vmem((SEQ, GROUP * HD), BF16),
            vmem((8, 8, HALF, HD), F32),
            vmem((8, 8, HALF, HD), F32),
            vmem((8, 4 * HALF + 16, HD), I16),
            vmem((8, 4 * HALF + 16, HD), I16),
            vmem((8, 3, HALF + 16, HD), I16),
            vmem((8, 3, HALF + 16, HD), I16),
            vmem((8, 3, 2, HALF, HD), BF16),
            vmem((8, 3, 2, HALF, HD), BF16),
            vmem((8, HALF, HD), BF16),
            vmem((8, HALF, HD), BF16),
            vmem((8, HALF, HD), F32),
            vmem((rows, HD), BF16),
            vmem((rows, HD), BF16),
            vmem((rows, wide), F32),
            vmem((rows, wide), F32),
            vmem((8, wide), F32),
            vmem((8, wide), F32),
            vmem((8, wide), F32),
            vmem((rows, wide), BF16),
            vmem((TILE, wide), BF16),
            vmem((4, TILE, HD), BF16),
            vmem((4, TILE, HD), BF16),
            vmem((4, 8, TILE, HD), BF16),
            vmem((4, 8, TILE, HD), BF16),
            vmem((4, 2, HALF, DEPTH), BF16),
            vmem((4, 2, HALF, DEPTH), BF16),
            vmem((TILE, DEPTH), F32),
            vmem((DEPTH, 4 * PITCH), BF16),
            pltpu.SMEM((4,), jnp.int32),
            vmem((1, SEQ), jnp.int32),
            dma((7,)), dma, dma, dma, dma((3, 2)),
            dma((8,)), dma((8,)), dma((6,)), dma((6,)), dma((8,)), dma((8,)),
            dma((4,)), dma((4, 2)), dma((4,)), dma((4,)), dma((4,)), dma((2,)), dma,
        ],
        compiler_params=pltpu.CompilerParams(
            collective_id=1, has_side_effects=True, vmem_limit_bytes=VMEM_LIMIT
        ),
        name="main",
    )(count, last, f, wk, wv, q, g)


PIECES = 2


def close_kernel(*refs):
    n = 4
    ins, outs, done = refs[:n], refs[n:2 * n], refs[2 * n]
    copies = []
    for i in range(n):
        rows = ins[i].shape[0] // PIECES
        for j in range(PIECES):
            part = pl.ds(j * rows, rows)
            copies.append(pltpu.make_async_copy(ins[i].at[part], outs[i].at[part], done.at[i, j]))
    for copy in copies:
        copy.start()
    for copy in copies:
        copy.wait()


def close(*arrays):
    n = len(arrays)
    return pl.pallas_call(
        close_kernel,
        out_shape=tuple(jax.ShapeDtypeStruct(x.shape, x.dtype) for x in arrays),
        in_specs=[pl.BlockSpec(memory_space=pltpu.VMEM)] * n,
        out_specs=(pl.BlockSpec(memory_space=pltpu.HBM),) * n,
        scratch_shapes=[pltpu.SemaphoreType.DMA((n, PIECES))],
        compiler_params=pltpu.CompilerParams(vmem_limit_bytes=8 * 2**20),
        name="close",
    )(*arrays)


def per_device(features, key_weight, value_weight, queries, out_grad, tile_count, tile_last):
    kgrad, vgrad, out, fgrad = close(*main(
        tile_count, tile_last.reshape(1, SEQ), features,
        key_weight[0], value_weight[0], queries[0], out_grad[0],
    ))
    return (out[None], fgrad, kgrad[None], vgrad[None])


def solution(mesh):
    in_specs = (
        P(("dp", "section"), "tensor"),
        P("section", "tensor", None),
        P("section", "tensor", None),
        P("section", "dp", "tensor"),
        P("section", "dp", "tensor"),
        P("dp"),
        P("dp"),
    )
    out_specs = (
        P("section", "dp", "tensor"),
        P(("dp", "section"), "tensor"),
        P("section", "tensor", "dp"),
        P("section", "tensor", "dp"),
    )
    return jax.shard_map(
        per_device, mesh=mesh, in_specs=in_specs, out_specs=out_specs, check_vma=False
    )
```

```python
import functools

import jax
import jax.numpy as jnp
from jax import lax
from jax.experimental import pallas as pl
from jax.experimental.pallas import tpu as pltpu
from jax.sharding import PartitionSpec as P

MESH = pl.DeviceIdType.MESH
F32 = jnp.float32
BF16 = jnp.bfloat16
I16 = jnp.int16
HD = 128
GROUP = 8
SECTIONS = 4
RING = 4
TILE = 192
HALF = TILE // 2
PITCH = 256
DEPTH = 1024
SEQ = 256
LEVELS = 32700.0
FLOOR = -1e30
VMEM_LIMIT = 58 * 2**20


def place():
    t = lax.axis_index("tensor")
    return lax.axis_index("section"), lax.axis_index("dp"), t // 2, lax.rem(t, 2)


def along_x(d):
    s, dp, y, z = place()
    return (lax.rem(s + d, SECTIONS), dp, y * 2 + z)


def along_y(d):
    s, dp, y, z = place()
    return (s, dp, lax.rem(y + d, RING) * 2 + z)


def along_z():
    s, dp, y, z = place()
    return (s, dp, y * 2 + (1 - z))


def greet():
    barrier = pltpu.get_barrier_semaphore()
    peers = [along_x(d) for d in (1, 3)] + [along_y(d) for d in (1, 2, 3)] + [along_z()]
    for peer in peers:
        pl.semaphore_signal(barrier, inc=1, device_id=peer, device_id_type=MESH)
    return barrier, len(peers)


def remote(src, dst, send_sem, recv_sem, device):
    return pltpu.make_async_remote_copy(
        src_ref=src, dst_ref=dst, send_sem=send_sem, recv_sem=recv_sem,
        device_id=device, device_id_type=MESH,
    )


def encode(x):
    top = jnp.maximum(jnp.max(jnp.abs(x), axis=0, keepdims=True), 1e-30)
    power = jnp.ceil(jnp.log(top) * 1.4426950408889634 + 0.0005)
    code = jnp.round(x * (jnp.exp2(-power) * LEVELS)).astype(jnp.int32).astype(I16)
    return code, power


def marks(powers):
    row = lax.broadcasted_iota(jnp.int32, (16, HD), 0)
    mark = jnp.broadcast_to(powers[0], (16, HD))
    for i, power in enumerate(powers[1:]):
        mark = jnp.where(row == i + 1, power, mark)
    return mark.astype(jnp.int32).astype(I16)


def units(mark):
    return jnp.exp2(mark.astype(jnp.int32).astype(F32)) * (1.0 / LEVELS)


def as_f32(code):
    return code.astype(jnp.int32).astype(F32)


ACROSS = (((1,), (1,)), ((), ()))
CHUNKS = ((0, 0), (0, 1), (1, 0), (3, 0), (1, 1), (3, 1), (2, 0), (2, 1))
UNITS = (((2, 0), (2, 1)), ((1, 0), (3, 0)), ((1, 1), (3, 1)), ((0, 0), (0, 1)))
ROWS = sum(UNITS, ())
RELAYED = 6
SLOT = {1: 0, 3: 1, 2: 2}


def ahead_of(i):
    return 1 if i % 2 == 0 else 3


def main_kernel(
    count_hbm, last_hbm, f_ref, wk_ref, wv_ref, q_ref, g_ref,
    kgrad, vgrad, att, fgrad,
    fg, wk, wv, q, g, pk, pv, kz_out, kz_in, ky_out, ky_in, vy_out, vy_in, vz_out, vz_in, sv,
    keys, values, expo, dprobs, tops, sums, dots, probs, dscores, dks, dvs, gk, gv, fs, fr, acc,
    ft, count, last,
    load, out1, out3, x_out, x_in, kz_sem, v1_sem, v2_sem, k1_sem, k2_sem, vz_sem,
    az_sem, by_sem, b2_sem, a2_sem, a3_sem, over_sem, part_sem,
):
    s, dp, y, z = place()
    scale = HD ** -0.5
    loads = [
        pltpu.make_async_copy(src, dst, load.at[i])
        for i, (src, dst) in enumerate((
            (f_ref, fg.at[0]), (wv_ref, wv), (wk_ref, wk), (q_ref, q), (g_ref, g),
            (last_hbm, last), (count_hbm, count),
        ))
    ]
    for copy in loads:
        copy.start()
    barrier, peers = greet()

    def go(*args):
        remote(*args).start()

    def done(ref, sem):
        pltpu.make_async_copy(ref, ref, sem).wait()

    def half(k, h):
        return fg.at[k, pl.ds(h * HALF, HALF)]

    def pass_x(k, h, to, d, sem):
        go(half(k, h), half(to, h), sem, x_in.at[to - 1, h], along_x(d))

    def head_at(d, r):
        return lax.rem(y + d, RING) * 2 + lax.rem(z + r, 2)

    def compute_v(i):
        k, h = CHUNKS[i]
        v = jnp.dot(fg[k, h * HALF:(h + 1) * HALF, :], wv[...], preferred_element_type=F32)
        for head in range(8):
            pv[i, head] = v[:, head * HD:(head + 1) * HD]
        for d in (2, RING - ahead_of(i)) if i < RELAYED else (2, 1, 3):
            for r in range(2):
                vy_out[i, SLOT[d], r] = pv[i, head_at(d, r)].astype(BF16)

    def compute_k(i):
        k, h = CHUNKS[i]
        p = jnp.dot(fg[k, h * HALF:(h + 1) * HALF, :], wk[...], preferred_element_type=F32)
        for head in range(8):
            pk[i, head] = p[:, head * HD:(head + 1) * HD]
        powers = []
        for d in range(RING):
            code, power = encode(pk[i, head_at(d, 1)])
            kz_out[i, d * HALF:(d + 1) * HALF, :] = code
            powers.append(power)
        kz_out[i, 4 * HALF:4 * HALF + 16, :] = marks(powers)

    def send_y(i, d, to, at, sem):
        go(vy_out.at[i, SLOT[d]], vy_in.at[i, SLOT[at]], out1, sem.at[i], along_y(to))

    def send_v(i):
        ahead = ahead_of(i)
        if i < RELAYED:
            send_y(i, 2, ahead, 2, v1_sem)
            send_y(i, RING - ahead, RING - ahead, ahead, v2_sem)
        else:
            for d in (2, 1, 3):
                send_y(i, d, d, RING - d, v1_sem)

    def send_z(i):
        go(kz_out.at[i], kz_in.at[i], out1, kz_sem.at[i], along_z())

    def start(i):
        k, h = CHUNKS[i]
        if k == 2:
            done(half(k, h), x_in.at[k - 1, h])
        compute_v(i)
        send_v(i)
        compute_k(i)
        send_z(i)

    def send_k(i, d, to, at, total, sem):
        code, power = encode(total)
        ky_out[i, SLOT[d], 0:HALF, :] = code
        ky_out[i, SLOT[d], HALF:HALF + 16, :] = marks([power])
        go(ky_out.at[i, SLOT[d]], ky_in.at[i, SLOT[at]], out1, sem.at[i], along_y(to))

    def got_k(i, at):
        unit = units(ky_in[i, at, HALF:HALF + 16, :])
        return as_f32(ky_in[i, at, 0:HALF, :]) * unit[0:1]

    def gather_v(i, n, sem):
        done(vy_in.at[i, pl.ds(0, n)], sem.at[i])
        for r in (1, 0):
            total = pv[i, head_at(0, r)]
            for at in range(n):
                total = total + vy_in[i, at, r].astype(F32)
            if r:
                vz_out[i] = total.astype(BF16)
                go(vz_out.at[i], vz_in.at[i], out1, vz_sem.at[i], along_z())
            else:
                sv[i] = total

    def middle(i):
        ahead = ahead_of(i)
        behind = RING - ahead
        if i < RELAYED:
            done(vy_in.at[i, 2], v1_sem.at[i])
            for r in range(2):
                total = pv[i, head_at(ahead, r)] + vy_in[i, 2, r].astype(F32)
                vy_out[i, SLOT[ahead], r] = total.astype(BF16)
            send_y(i, ahead, ahead, behind, v2_sem)
        done(kz_in.at[i], kz_sem.at[i])
        unit = units(kz_in[i, 4 * HALF:4 * HALF + 16, :])
        for d in (2, 1, 3, 0):
            head = head_at(d, 0)
            total = pk[i, head] + as_f32(kz_in[i, d * HALF:(d + 1) * HALF, :]) * unit[d:d + 1]
            if i >= RELAYED and d:
                send_k(i, d, d, RING - d, total, k2_sem)
            elif d == 2:
                send_k(i, 2, behind, 2, total, k1_sem)
            elif d == ahead:
                send_k(i, ahead, ahead, behind, total, k2_sem)
            else:
                pk[i, head] = total
        if i >= RELAYED:
            gather_v(i, 3, v1_sem)

    def relay(i):
        ahead = ahead_of(i)
        behind = RING - ahead
        done(ky_in.at[i, 2], k1_sem.at[i])
        send_k(i, behind, behind, ahead, pk[i, head_at(behind, 0)] + got_k(i, 2), k2_sem)
        gather_v(i, 2, v2_sem)

    def finish(i):
        k, h = CHUNKS[i]
        at = ROWS.index((k, h)) * HALF
        spot = slice(at, at + HALF)
        n = 2 if i < RELAYED else 3
        done(ky_in.at[i, pl.ds(0, n)], k2_sem.at[i])
        total = pk[i, head_at(0, 0)]
        for at in range(n):
            total = total + got_k(i, at)
        key = total.astype(BF16)
        keys[spot, :] = key
        done(vz_in.at[i], vz_sem.at[i])
        value = (sv[i] + vz_in[i].astype(F32)).astype(BF16)
        values[spot, :] = value
        tile = lax.rem(s + k, SECTIONS)
        slot = lax.broadcasted_iota(jnp.int32, (HALF, SEQ), 0) + h * HALF
        limit = jnp.where(slot < count[tile], tile, SECTIONS)
        visible = limit <= last[...]
        for j in range(GROUP):
            cols = slice(j * HD, (j + 1) * HD)
            wide = slice(j * SEQ, (j + 1) * SEQ)
            scores = lax.dot_general(key, q[:, cols], ACROSS, preferred_element_type=F32) * scale
            masked = jnp.where(visible, scores, -jnp.inf)
            top = jnp.maximum(jnp.max(masked, axis=0, keepdims=True), FLOOR)
            e = jnp.exp(masked - top)
            dprob = lax.dot_general(value, g[:, cols], ACROSS, preferred_element_type=F32)
            expo[spot, wide] = e
            dprobs[spot, wide] = dprob
            tops[i:i + 1, wide] = top
            sums[i:i + 1, wide] = jnp.sum(e, axis=0, keepdims=True)
            dots[i:i + 1, wide] = jnp.sum(e * dprob, axis=0, keepdims=True)

    def turn(k):
        rows = [fg[tile, h * HALF:(h + 1) * HALF, :] for tile, h in UNITS[k]]
        ft[:, k * PITCH:k * PITCH + TILE] = jnp.concatenate(rows, axis=0).T

    loads[0].wait()
    loads[1].wait()
    compute_v(0)
    pl.semaphore_wait(barrier, peers)
    pass_x(0, 0, 3, 1, x_out)
    pass_x(0, 0, 1, 3, x_out)
    send_v(0)
    loads[2].wait()
    compute_k(0)
    send_z(0)
    start(1)
    middle(0)
    done(fg.at[0], x_out)
    pass_x(0, 1, 3, 1, out1)
    pass_x(0, 1, 1, 3, out1)
    middle(1)
    done(half(1, 0), x_in.at[0, 0])
    start(2)
    done(half(3, 0), x_in.at[2, 0])
    start(3)
    relay(0)
    relay(1)
    for copy in loads[3:]:
        copy.wait()
    done(half(1, 1), x_in.at[0, 1])
    pass_x(1, 0, 2, 3, out1)
    done(half(3, 1), x_in.at[2, 1])
    pass_x(3, 1, 2, 1, out1)
    start(4)
    middle(2)
    start(5)
    middle(3)
    relay(2)
    finish(0)
    finish(1)
    start(6)
    middle(4)
    relay(3)
    start(7)
    middle(5)
    relay(4)
    finish(2)
    middle(6)
    relay(5)
    finish(3)
    middle(7)
    finish(4)
    for k in range(4):
        turn(k)
    finish(5)
    finish(6)
    finish(7)

    peak = jnp.max(tops[...], axis=0, keepdims=True)
    share = jnp.exp(tops[...] - peak)
    inverse = 1.0 / jnp.sum(share * sums[...], axis=0, keepdims=True)
    share = share * inverse
    sums[...] = share
    dots[0:1, :] = jnp.sum(share * dots[...], axis=0, keepdims=True)

    mine = y * 2 + z

    def heads(ref, k):
        return jnp.concatenate([ref[k, head] for head in range(8)], axis=1)

    def attend(k):
        dk = dv = None
        for j in range(GROUP):
            narrow = slice(j * HD, (j + 1) * HD)
            wide = slice(j * SEQ, (j + 1) * SEQ)
            delta = dots[0:1, wide]
            for h in range(2):
                i = CHUNKS.index(UNITS[k][h])
                spot = slice(k * TILE + h * HALF, k * TILE + (h + 1) * HALF)
                p = expo[spot, wide] * sums[i:i + 1, wide]
                probs[spot, wide] = p.astype(BF16)
                dscores[h * HALF:(h + 1) * HALF, wide] = (p * (dprobs[spot, wide] - delta) * scale).astype(BF16)
            whole = slice(k * TILE, (k + 1) * TILE)
            dv_j = jnp.dot(probs[whole, wide], g[:, narrow], preferred_element_type=F32)
            dk_j = jnp.dot(dscores[:, wide], q[:, narrow], preferred_element_type=F32)
            dv = dv_j if j == 0 else dv + dv_j
            dk = dk_j if j == 0 else dk + dk_j
        for ref, into, value in ((dvs, gv, dv), (dks, gk, dk)):
            rounded = value.astype(BF16)
            ref[k] = rounded
            into[k, mine] = rounded

    def ways(k):
        return (1, 3) if k % 2 == 0 else (3, 1)

    def zero(k):
        for d in (1, 3):
            go(dvs.at[k], gv.at[k, mine], out3, by_sem.at[k, SLOT[RING - d]], along_y(d))
        go(dks.at[k], gk.at[k, mine], out3, az_sem.at[k], along_z())
        go(dvs.at[k], gv.at[k, mine], out3, a3_sem.at[k], along_z())

    def one(k):
        ahead, behind = ways(k)
        done(gk.at[k, 0], az_sem.at[k])
        pair = pl.ds(y * 2, 2)
        go(gk.at[k, pair], gk.at[k, pair], out3, a2_sem.at[k], along_y(ahead))
        go(gk.at[k, pair], gk.at[k, pair], out3, a3_sem.at[k], along_y(behind))
        for d in (behind, ahead):
            done(gv.at[k, 0], by_sem.at[k, SLOT[d]])
            head = head_at(d, 0)
            if d == behind:
                go(gv.at[k, head], gv.at[k, head], out3, b2_sem.at[k], along_y(ahead))
            go(gv.at[k, head], gv.at[k, head], out3, a3_sem.at[k], along_z())

    def two(k):
        ahead, behind = ways(k)
        done(gk.at[k, pl.ds(0, 2)], a2_sem.at[k])
        pair = pl.ds(lax.rem(y + behind, RING) * 2, 2)
        go(gk.at[k, pair], gk.at[k, pair], out3, a3_sem.at[k], along_y(ahead))
        done(gv.at[k, 0], b2_sem.at[k])
        head = head_at(2, 0)
        go(gv.at[k, head], gv.at[k, head], out3, a3_sem.at[k], along_z())

    def three(k):
        done(gk.at[k], a3_sem.at[k])
        total = lax.dot_general(heads(gk, k), wk[...], ACROSS, preferred_element_type=F32)
        total += lax.dot_general(heads(gv, k), wv[...], ACROSS, preferred_element_type=F32)
        for h, (tile, part) in enumerate(UNITS[k]):
            half_total = total[h * HALF:(h + 1) * HALF]
            if tile == 0:
                acc[h * HALF:(h + 1) * HALF, :] = half_total
                continue
            way = tile if tile != 2 else (3, 1)[part]
            if (tile, part) in ((1, 1), (3, 0)):
                done(fr.at[2, part], over_sem.at[part])
                half_total = half_total + fr[2, part].astype(F32)
            fs[tile, part] = half_total.astype(BF16)
            if tile == 2:
                go(fs.at[tile, part], fr.at[2, part], out3, over_sem.at[part], along_x(way))
            else:
                go(fs.at[tile, part], fr.at[SLOT[SECTIONS - way], part], out3, part_sem, along_x(way))

    def weights(k):
        for j, (src, dst) in enumerate(((gk, kgrad), (gv, vgrad))):
            side = slice(j * DEPTH, (j + 1) * DEPTH)
            total = jnp.dot(ft[:, k * PITCH:k * PITCH + TILE], heads(src, k), preferred_element_type=F32)
            for held, out in (
                (expo.at[0:3 * SEQ, side], slice(0, 3 * SEQ)),
                (dprobs.at[0:SEQ, side], slice(3 * SEQ, 4 * SEQ)),
            ):
                if k == 0:
                    held[...] = total[out]
                elif k < 3:
                    held[...] += total[out]
                else:
                    dst[out, :] = (held[...] + total[out]).astype(BF16)

    def forward():
        turned = values[...].T
        for j in range(GROUP):
            out = jnp.dot(turned, probs[:, j * SEQ:(j + 1) * SEQ], preferred_element_type=F32)
            att[:, j * HD:(j + 1) * HD] = out.T.astype(BF16)

    attend(0)
    zero(0)
    attend(1)
    zero(1)
    one(0)
    attend(2)
    zero(2)
    one(1)
    two(0)
    attend(3)
    zero(3)
    one(2)
    two(1)
    three(0)
    one(3)
    two(2)
    forward()
    weights(0)
    two(3)
    three(1)
    three(2)
    three(3)
    weights(1)
    weights(2)
    weights(3)
    done(fr.at[pl.ds(0, 2)], part_sem)
    for h in range(2):
        rows = slice(h * HALF, (h + 1) * HALF)
        total = acc[rows, :]
        for at in (0, 1):
            total = total + fr[at, h].astype(F32)
        fgrad[rows, :] = total.astype(BF16)
    done(expo.at[pl.ds(0, 448)], out1)
    done(expo.at[pl.ds(0, 480)], out3)


def main(count, last, f, wk, wv, q, g):
    dma = pltpu.SemaphoreType.DMA
    vmem = pltpu.VMEM
    held = pl.BlockSpec(memory_space=pltpu.HBM)
    rows = 4 * TILE
    wide = GROUP * SEQ
    return pl.pallas_call(
        main_kernel,
        out_shape=(
            vmem((DEPTH, GROUP * HD), BF16),
            vmem((DEPTH, GROUP * HD), BF16),
            vmem((SEQ, GROUP * HD), BF16),
            vmem((TILE, DEPTH), BF16),
        ),
        in_specs=[held] * 7,
        out_specs=(pl.BlockSpec(memory_space=pltpu.VMEM),) * 4,
        scratch_shapes=[
            vmem((4, TILE, DEPTH), BF16),
            vmem((DEPTH, GROUP * HD), BF16),
            vmem((DEPTH, GROUP * HD), BF16),
            vmem((SEQ, GROUP * HD), BF16),
            vmem((SEQ, GROUP * HD), BF16),
            vmem((8, 8, HALF, HD), F32),
            vmem((8, 8, HALF, HD), F32),
            vmem((8, 4 * HALF + 16, HD), I16),
            vmem((8, 4 * HALF + 16, HD), I16),
            vmem((8, 3, HALF + 16, HD), I16),
            vmem((8, 3, HALF + 16, HD), I16),
            vmem((8, 3, 2, HALF, HD), BF16),
            vmem((8, 3, 2, HALF, HD), BF16),
            vmem((8, HALF, HD), BF16),
            vmem((8, HALF, HD), BF16),
            vmem((8, HALF, HD), F32),
            vmem((rows, HD), BF16),
            vmem((rows, HD), BF16),
            vmem((rows, wide), F32),
            vmem((rows, wide), F32),
            vmem((8, wide), F32),
            vmem((8, wide), F32),
            vmem((8, wide), F32),
            vmem((rows, wide), BF16),
            vmem((TILE, wide), BF16),
            vmem((4, TILE, HD), BF16),
            vmem((4, TILE, HD), BF16),
            vmem((4, 8, TILE, HD), BF16),
            vmem((4, 8, TILE, HD), BF16),
            vmem((4, 2, HALF, DEPTH), BF16),
            vmem((4, 2, HALF, DEPTH), BF16),
            vmem((TILE, DEPTH), F32),
            vmem((DEPTH, 4 * PITCH), BF16),
            pltpu.SMEM((4,), jnp.int32),
            vmem((1, SEQ), jnp.int32),
            dma((7,)), dma, dma, dma, dma((3, 2)),
            dma((8,)), dma((8,)), dma((6,)), dma((6,)), dma((8,)), dma((8,)),
            dma((4,)), dma((4, 2)), dma((4,)), dma((4,)), dma((4,)), dma((2,)), dma,
        ],
        compiler_params=pltpu.CompilerParams(
            collective_id=1, has_side_effects=True, vmem_limit_bytes=VMEM_LIMIT
        ),
        name="main",
    )(count, last, f, wk, wv, q, g)


PIECES = 2


def close_kernel(*refs):
    n = 4
    ins, outs, done = refs[:n], refs[n:2 * n], refs[2 * n]
    copies = []
    for i in range(n):
        rows = ins[i].shape[0] // PIECES
        for j in range(PIECES):
            part = pl.ds(j * rows, rows)
            copies.append(pltpu.make_async_copy(ins[i].at[part], outs[i].at[part], done.at[i, j]))
    for copy in copies:
        copy.start()
    for copy in copies:
        copy.wait()


def close(*arrays):
    n = len(arrays)
    return pl.pallas_call(
        close_kernel,
        out_shape=tuple(jax.ShapeDtypeStruct(x.shape, x.dtype) for x in arrays),
        in_specs=[pl.BlockSpec(memory_space=pltpu.VMEM)] * n,
        out_specs=(pl.BlockSpec(memory_space=pltpu.HBM),) * n,
        scratch_shapes=[pltpu.SemaphoreType.DMA((n, PIECES))],
        compiler_params=pltpu.CompilerParams(vmem_limit_bytes=8 * 2**20),
        name="close",
    )(*arrays)


def per_device(features, key_weight, value_weight, queries, out_grad, tile_count, tile_last):
    kgrad, vgrad, out, fgrad = close(*main(
        tile_count, tile_last.reshape(1, SEQ), features,
        key_weight[0], value_weight[0], queries[0], out_grad[0],
    ))
    return (out[None], fgrad, kgrad[None], vgrad[None])


def solution(mesh):
    in_specs = (
        P(("dp", "section"), "tensor"),
        P("section", "tensor", None),
        P("section", "tensor", None),
        P("section", "dp", "tensor"),
        P("section", "dp", "tensor"),
        P("dp"),
        P("dp"),
    )
    out_specs = (
        P("section", "dp", "tensor"),
        P(("dp", "section"), "tensor"),
        P("section", "tensor", "dp"),
        P("section", "tensor", "dp"),
    )
    return jax.shard_map(
        per_device, mesh=mesh, in_specs=in_specs, out_specs=out_specs, check_vma=False
    )
```
